512 devices in a mesh: gx: 16 (over z), gz: 32 (over y, x, core).
Axes of the slice: x: 4, y: 4, z: 16, core: 2. Of those that a mesh axis runs over, the one named last changes fastest.
Arguments:
- velocity: float32 [3, 4, 2048, 2048], P(None, None, 'gz', 'gx'), may hold values from -6 to 6
- old_rhs: float32 [3, 4, 2048, 2048], P(None, None, 'gz', 'gx'), may hold values from -6 to 6
Outputs:
- new_velocity: float32 [3, 4, 2048, 2048], P(None, None, 'gz', 'gx')
- rhs: float32 [3, 4, 2048, 2048], P(None, None, 'gz', 'gx')
The draws below stay inside these ranges and needn't reach their ends.
All inputs are finite; a program needn't handle non-finite values.
Results may differ from the reference program's by a relative error of at most 0.0001.
Values sent between devices are 32-bit elements; how exact they have to be, the bound alone decides.
No kernel may reach another device: no remote copies, remote signals or barrier semaphores. Data moves between devices by JAX's collectives and lax.ppermute only.
A program may use at most 64 MiB of HBM per device.

```python
import math
import jax
import jax.numpy as jnp

YW = 4
NX = 2048
NZ = 2048


def levels(key, extent, shards, least, high):
    level = 1.0
    for dim, shards_of in shards:
        heights = jax.random.uniform(jax.random.fold_in(jax.random.fold_in(key, 6), dim), (shards_of,), jnp.float32, least / len(shards), high / len(shards))
        level = level * jnp.repeat(jnp.exp(heights), extent[dim] // shards_of).reshape((-1,) + (1,) * (len(extent) - 1 - dim))
    return level


def centred(key, dims, scale, limit, cuts=(), kind=jnp.bfloat16):
    gain = levels(key, dims, cuts, -0.22, 0.18) if cuts else 1.0
    entries = jax.random.normal(key, dims, jnp.float32) * scale * gain
    return jnp.minimum(jnp.maximum(entries, -limit), limit).astype(kind)


def setup_inputs(seed: int = 0) -> dict:
    key_of = jax.random.split(jax.random.key(seed), 3)
    return {
        "velocity": centred(key_of[0], (3, YW, NZ, NX), 1.0, 6.0, ((2, 32), (3, 16)), jnp.float32),
        "old_rhs": centred(key_of[1], (3, YW, NZ, NX), 1.0, 6.0, ((2, 32), (3, 16)), jnp.float32),
    }


first_alpha = 1.0 / 3.0
first_near = 14.0 / 9.0
first_far = 1.0 / 9.0
second_alpha = 2.0 / 11.0
second_near = 12.0 / 11.0
second_far = 3.0 / 11.0
viscosity = 0.2
time_step = 0.25
gamma_now = 5.0 / 12.0
zeta_old = -17.0 / 60.0


def wave_numbers(length):
    return 2.0 * math.pi * jnp.arange(length // 2 + 1, dtype=jnp.float32) / length


def stream_first(field_in):
    length = field_in.shape[-1]
    wavenumber = wave_numbers(length)
    symbol = (first_near * jnp.sin(wavenumber) + 0.5 * first_far * jnp.sin(2.0 * wavenumber)) / (1.0 + 2.0 * first_alpha * jnp.cos(wavenumber))
    spectrum = jnp.fft.rfft(field_in, axis=-1)
    return jnp.fft.irfft(spectrum * (1j * symbol), n=length, axis=-1).astype(jnp.float32)


def stream_second(field_in):
    length = field_in.shape[-1]
    wavenumber = wave_numbers(length)
    symbol = (2.0 * second_near * (jnp.cos(wavenumber) - 1.0) + 0.5 * second_far * (jnp.cos(2.0 * wavenumber) - 1.0)) / (1.0 + 2.0 * second_alpha * jnp.cos(wavenumber))
    spectrum = jnp.fft.rfft(field_in, axis=-1)
    return jnp.fft.irfft(spectrum * symbol, n=length, axis=-1).astype(jnp.float32)


def span_shift(field_in, offset):
    return jnp.roll(field_in, -offset, axis=-2)


def span_first(field_in):
    return (45.0 * (span_shift(field_in, 1) - span_shift(field_in, -1)) - 9.0 * (span_shift(field_in, 2) - span_shift(field_in, -2)) + (span_shift(field_in, 3) - span_shift(field_in, -3))) / 60.0


def span_second(field_in):
    return (2.0 * (span_shift(field_in, 3) + span_shift(field_in, -3)) - 27.0 * (span_shift(field_in, 2) + span_shift(field_in, -2)) + 270.0 * (span_shift(field_in, 1) + span_shift(field_in, -1)) - 490.0 * field_in) / 180.0


def reference(velocity, old_rhs):
    new_list = []
    rhs_list = []
    for plane_index in range(YW):
        plane_vel = velocity[:, plane_index]
        stream_vel = plane_vel[0][None]
        span_vel = plane_vel[2][None]
        flux_x = stream_vel * plane_vel
        flux_z = span_vel * plane_vel
        advect = stream_vel * stream_first(plane_vel) + span_vel * span_first(plane_vel) + stream_first(flux_x) + span_first(flux_z)
        right_side = -0.5 * advect + viscosity * (stream_second(plane_vel) + span_second(plane_vel))
        new_list.append(plane_vel + time_step * (gamma_now * right_side + zeta_old * old_rhs[:, plane_index]))
        rhs_list.append(right_side)
    return jnp.stack(new_list, 1), jnp.stack(rhs_list, 1)
```

```python
import math

import jax
import jax.numpy as jnp
import ml_dtypes
import numpy as np
from jax import lax
from jax.experimental import pallas as pl
from jax.experimental.pallas import tpu as pltpu
from jax.sharding import PartitionSpec as P

first_alpha = 1.0 / 3.0
first_near = 14.0 / 9.0
first_far = 1.0 / 9.0
second_alpha = 2.0 / 11.0
second_near = 12.0 / 11.0
second_far = 3.0 / 11.0
viscosity = 0.2
time_step = 0.25
gamma_now = 5.0 / 12.0
zeta_old = -17.0 / 60.0
first_stencil = (
    (1, 0.5 * first_near),
    (-1, -0.5 * first_near),
    (2, 0.25 * first_far),
    (-2, -0.25 * first_far),
)
second_stencil = (
    (0, -2.0 * second_near - 0.5 * second_far),
    (1, second_near),
    (-1, second_near),
    (2, 0.25 * second_far),
    (-2, 0.25 * second_far),
)
span_odd = (45.0 / 60.0, -9.0 / 60.0, 1.0 / 60.0)
span_even = (270.0 / 180.0, -27.0 / 180.0, 2.0 / 180.0)
span_centre = -490.0 / 180.0


def green(off_diag):
    root = (-1.0 + math.sqrt(1.0 - 4.0 * off_diag * off_diag)) / (2.0 * off_diag)
    return root, 1.0 / (1.0 + 2.0 * off_diag * root)


def weight_at(distance, stencil, off_diag):
    root, lead = green(off_diag)
    return sum(w * lead * root ** np.abs(distance + o) for o, w in stencil)


def reach_of(stencil, off_diag):
    root, lead = green(off_diag)
    return lead * sum(w * root**o for o, w in stencil)


def split_np(matrix):
    high = matrix.astype(ml_dtypes.bfloat16)
    low = (matrix - high.astype(np.float64)).astype(ml_dtypes.bfloat16)
    return high, low


def block_matrix(stencil, off_diag, extent):
    ids = np.arange(extent)
    return weight_at(ids[None, :] - ids[:, None], stencil, off_diag)


def inner_tables(extent):
    tables = []
    for stencil, off_diag in ((first_stencil, first_alpha), (second_stencil, second_alpha)):
        high, low = split_np(block_matrix(stencil, off_diag, extent))
        half = np.concatenate([high, low], 1)
        tables.append(np.concatenate([half, half], 0))
    return tables


def moment_table(extent):
    ids = np.arange(extent)
    rows = np.zeros((8, extent))
    for side, away in ((0, ids), (1, extent - 1 - ids)):
        rows[3 * side] = green(first_alpha)[0] ** away
        rows[3 * side + 1] = green(second_alpha)[0] ** away
        rows[3 * side + 2] = away == 0
    return rows.astype(np.float32)


def outer_table(extent):
    ids = np.arange(extent)
    table = np.zeros((16, 2 * extent))
    for side, away, sign in ((0, ids + 1, 1.0), (1, extent - ids, -1.0)):
        root1, root2 = green(first_alpha)[0], green(second_alpha)[0]
        far1 = reach_of(first_stencil, first_alpha) * root1**away
        far2 = reach_of(second_stencil, second_alpha) * root2**away
        near1 = (weight_at(np.array(1), first_stencil, first_alpha) - far1) * (away == 1)
        near2 = (weight_at(np.array(1), second_stencil, second_alpha) - far2) * (away == 1)
        row = 5 * side
        table[row, :extent] = sign * far1
        table[row + 1, extent:] = viscosity * far2
        table[row + 2, :extent] = sign * near1
        table[row + 2, extent:] = viscosity * near2
        table[row + 3, extent:] = -0.5 * sign * far1
        table[row + 4, extent:] = -0.5 * sign * near1
    high, low = split_np(table)
    return np.concatenate([high, high, low], 0)


def split(values):
    high = values.astype(jnp.bfloat16)
    low = (values - high.astype(jnp.float32)).astype(jnp.bfloat16)
    return high, low


def moments_kernel(vel_ref, table_ref, lower_ref, upper_ref):
    planes, rows, cols = vel_ref.shape[1:]
    lines = planes * rows
    nt = (((1,), (1,)), ((), ()))
    u = vel_ref[0].reshape(lines, cols)
    table = table_ref[...]
    for i in range(3):
        v = vel_ref[i].reshape(lines, cols)
        got = lax.dot_general(table, v, nt, precision=lax.Precision.HIGHEST, preferred_element_type=jnp.float32)
        flux = lax.dot_general(table, u * v, nt, precision=lax.Precision.HIGHEST, preferred_element_type=jnp.float32)
        at = slice(i * lines, (i + 1) * lines)
        lower_ref[0:3, at] = got[0:3]
        lower_ref[3:4, at] = flux[0:1]
        upper_ref[0:3, at] = got[3:6]
        upper_ref[3:4, at] = flux[3:4]


def mul_split(values, table):
    high, low = split(values)
    got = jnp.dot(jnp.concatenate([high, low], 1), table, preferred_element_type=jnp.float32)
    half = table.shape[1] // 2
    return got[:, :half] + got[:, half:]


def shifted(values, offset):
    planes, rows, cols = values.shape
    zeros = jnp.zeros((planes, abs(offset), cols), values.dtype)
    if offset > 0:
        return jnp.concatenate([values[:, offset:], zeros], 1)
    return jnp.concatenate([zeros, values[:, :offset]], 1)


def span_tap(v_far, w_near, w_far, distance, sign):
    odd = -0.5 * sign * span_odd[distance - 1]
    even = viscosity * span_even[distance - 1]
    return v_far * (odd * (w_near + w_far) + even)


def inner_kernel(vel_ref, first_ref, second_ref, part_ref):
    planes, rows, cols = vel_ref.shape[1:]
    lines = planes * rows
    u = vel_ref[0].reshape(lines, cols)
    w = vel_ref[2]
    for i in range(3):
        v3 = vel_ref[i]
        v = v3.reshape(lines, cols)
        slope = mul_split(v, first_ref[...])
        curve = mul_split(v, second_ref[...])
        flux = mul_split(u * v, first_ref[...])
        total = -0.5 * (u * slope + flux) + viscosity * curve
        total = total.reshape(planes, rows, cols) + (viscosity * span_centre) * v3
        for distance in (1, 2, 3):
            for sign in (1, -1):
                offset = sign * distance
                total = total + span_tap(shifted(v3, offset), w, shifted(w, offset), distance, sign)
        part_ref[i] = total


def outer_kernel(vel_ref, old_ref, part_ref, left_ref, right_ref, below_ref, above_ref, table_ref, new_ref, rhs_ref):
    planes, rows, cols = vel_ref.shape[1:]
    lines = planes * rows
    u = vel_ref[0].reshape(lines, cols)
    w = vel_ref[2]
    u_edge = (left_ref[2:3, :lines], right_ref[2:3, :lines])
    tn = (((0,), (0,)), ((), ()))
    for i in range(3):
        at = slice(i * lines, (i + 1) * lines)
        pieces = []
        for side, ref in ((0, left_ref), (1, right_ref)):
            got = ref[:, at]
            pieces += [got, got[2:3] * u_edge[side]]
        pieces.append(jnp.zeros((6, lines), jnp.float32))
        high, low = split(jnp.concatenate(pieces, 0))
        spread = lax.dot_general(
            jnp.concatenate([high, low, high], 0), table_ref[...], tn, preferred_element_type=jnp.float32
        )
        total = part_ref[i] + (spread[:, cols:] - 0.5 * u * spread[:, :cols]).reshape(planes, rows, cols)
        low_fix = jnp.zeros((planes, 8, cols), jnp.float32)
        high_fix = jnp.zeros((planes, 8, cols), jnp.float32)
        for d in (1, 2, 3):
            pad = jnp.zeros((planes, 8 - d, cols), jnp.float32)
            v_far = jnp.concatenate([below_ref[i, :, 3 - d :], pad], 1)
            w_far = jnp.concatenate([below_ref[2, :, 3 - d :], pad], 1)
            low_fix = low_fix + span_tap(v_far, w[:, :8], w_far, d, -1)
            v_far = jnp.concatenate([pad, above_ref[i, :, :d]], 1)
            w_far = jnp.concatenate([pad, above_ref[2, :, :d]], 1)
            high_fix = high_fix + span_tap(v_far, w[:, rows - 8 :], w_far, d, 1)
        total = jnp.concatenate(
            [total[:, :8] + low_fix, total[:, 8 : rows - 8], total[:, rows - 8 :] + high_fix], 1
        )
        rhs_ref[i] = total
        new_ref[i] = vel_ref[i] + (time_step * gamma_now) * total + (time_step * zeta_old) * old_ref[i]


def send(values, axis, step):
    count = lax.axis_size(axis)
    return lax.ppermute(values, axis, [(i, (i + step) % count) for i in range(count)])


def local(velocity, old_rhs):
    fields, planes, rows, cols = velocity.shape
    lines = planes * rows
    whole = pl.BlockSpec(memory_space=pltpu.VMEM)
    f32 = jnp.float32
    block = jax.ShapeDtypeStruct(velocity.shape, f32)
    side = jax.ShapeDtypeStruct((4, fields * lines), f32)
    params = pltpu.CompilerParams(vmem_limit_bytes=32 * 1024 * 1024)

    below = send(velocity[:, :, rows - 3 :], "gz", 1)
    above = send(velocity[:, :, :3], "gz", -1)
    lower, upper = pl.pallas_call(
        moments_kernel,
        out_shape=(side, side),
        in_specs=[whole] * 2,
        out_specs=(whole, whole),
        compiler_params=params,
        name="moments",
    )(velocity, jnp.asarray(moment_table(cols)))
    from_left = send(upper, "gx", 1)
    from_right = send(lower, "gx", -1)
    first, second = inner_tables(cols)
    part = pl.pallas_call(
        inner_kernel,
        out_shape=block,
        in_specs=[whole] * 3,
        out_specs=whole,
        compiler_params=params,
        cost_estimate=pl.CostEstimate(flops=600_000_000, bytes_accessed=1_000_000, transcendentals=0),
        name="inner",
    )(velocity, jnp.asarray(first), jnp.asarray(second))
    new_velocity, right_side = pl.pallas_call(
        outer_kernel,
        out_shape=(block, block),
        in_specs=[whole] * 8,
        out_specs=(whole, whole),
        compiler_params=params,
        name="outer",
    )(velocity, old_rhs, part, from_left, from_right, below, above, jnp.asarray(outer_table(cols)))
    return new_velocity, right_side


def solution(mesh):
    spec = P(None, None, "gz", "gx")
    return jax.shard_map(local, mesh=mesh, in_specs=(spec, spec), out_specs=(spec, spec), check_vma=False)
```

```python
import functools
import math

import jax
import jax.numpy as jnp
from jax import lax
from jax.experimental import pallas as pl
from jax.experimental.pallas import tpu as pltpu
from jax.sharding import PartitionSpec as P

first_alpha = 1.0 / 3.0
first_near = 14.0 / 9.0
first_far = 1.0 / 9.0
second_alpha = 2.0 / 11.0
second_near = 12.0 / 11.0
second_far = 3.0 / 11.0
viscosity = 0.2
time_step = 0.25
gamma_now = 5.0 / 12.0
zeta_old = -17.0 / 60.0
first_stencil = (
    (1, 0.5 * first_near),
    (-1, -0.5 * first_near),
    (2, 0.25 * first_far),
    (-2, -0.25 * first_far),
)
second_stencil = (
    (0, -2.0 * second_near - 0.5 * second_far),
    (1, second_near),
    (-1, second_near),
    (2, 0.25 * second_far),
    (-2, 0.25 * second_far),
)
span_odd = (45.0 / 60.0, -9.0 / 60.0, 1.0 / 60.0)
span_even = (270.0 / 180.0, -27.0 / 180.0, 2.0 / 180.0)
span_centre = -490.0 / 180.0


def green(off_diag):
    root = (-1.0 + math.sqrt(1.0 - 4.0 * off_diag * off_diag)) / (2.0 * off_diag)
    return root, 1.0 / (1.0 + 2.0 * off_diag * root)


def weight_at(distance, stencil, off_diag):
    root, lead = green(off_diag)
    return sum(w * lead * root ** abs(distance + o) for o, w in stencil)


def reach_of(stencil, off_diag):
    root, lead = green(off_diag)
    return lead * sum(w * root**o for o, w in stencil)


def decay(away, off_diag):
    power = jnp.exp(away.astype(jnp.float32) * math.log(-green(off_diag)[0]))
    return jnp.where((away & 1) == 1, -power, power)


def block_matrix(stencil, off_diag, extent, odd):
    row = lax.broadcasted_iota(jnp.int32, (extent, extent), 0)
    column = lax.broadcasted_iota(jnp.int32, (extent, extent), 1)
    away = jnp.abs(column - row)
    far = reach_of(stencil, off_diag) * decay(away, off_diag)
    weight = jnp.where(away == 0, weight_at(0, stencil, off_diag), jnp.where(away == 1, weight_at(1, stencil, off_diag), far))
    if odd:
        weight = jnp.where(column < row, -weight, weight)
    half = jnp.concatenate(split(weight), 1)
    return jnp.concatenate([half, half], 0)


def outer_table(extent):
    row = lax.broadcasted_iota(jnp.int32, (16, 2 * extent), 0)
    column = lax.broadcasted_iota(jnp.int32, (16, 2 * extent), 1)
    left = row < 5
    kind = jnp.where(left, row, row - 5)
    slope = column < extent
    cell = jnp.where(slope, column, column - extent)
    away = jnp.where(left, cell + 1, extent - cell)
    sign = jnp.where(left, 1.0, -1.0)
    reach1, reach2 = reach_of(first_stencil, first_alpha), reach_of(second_stencil, second_alpha)
    near1 = weight_at(1, first_stencil, first_alpha) - reach1 * green(first_alpha)[0]
    near2 = weight_at(1, second_stencil, second_alpha) - reach2 * green(second_alpha)[0]
    touch = (away == 1).astype(jnp.float32)
    far1 = sign * reach1 * decay(away, first_alpha)
    far2 = viscosity * reach2 * decay(away, second_alpha)
    slopes = jnp.where(kind == 0, far1, jnp.where(kind == 2, sign * near1 * touch, 0.0))
    rests = jnp.where(kind == 1, far2, jnp.where(kind == 2, viscosity * near2 * touch, 0.0))
    rests = jnp.where(kind == 3, -0.5 * far1, jnp.where(kind == 4, -0.5 * sign * near1 * touch, rests))
    high, low = split(jnp.where(slope, slopes, rests))
    return jnp.concatenate([high, high, low], 0)


def split(values):
    high = values.astype(jnp.bfloat16)
    low = (values - high.astype(jnp.float32)).astype(jnp.bfloat16)
    return high, low


def moments_kernel(vel_ref, held_ref, lower_ref, upper_ref, outward_ref, inward_ref, sems):
    fields, planes, rows, cols = vel_ref.shape
    lines = planes * rows
    copies = [pltpu.make_async_copy(vel_ref.at[i], held_ref.at[i], sems.at[i]) for i in range(fields)]
    for copy in copies:
        copy.start()
    row = lax.broadcasted_iota(jnp.int32, (8, cols), 0)
    cell = lax.broadcasted_iota(jnp.int32, (8, cols), 1)
    away = jnp.where(row < 3, cell, cols - 1 - cell)
    kind = jnp.where(row < 3, row, row - 3)
    power = jnp.where(kind == 0, decay(away, first_alpha), decay(away, second_alpha))
    table = jnp.where(kind == 2, (away == 0).astype(jnp.float32), jnp.where(kind > 2, 0.0, power))
    high, low = split(table)
    both = jnp.concatenate([high, low], 0)
    odd = lax.rem(lax.axis_index("gz"), 2)
    nt = (((1,), (1,)), ((), ()))

    def moments(values):
        first, second = split(values)
        got = lax.dot_general(both, first, nt, preferred_element_type=jnp.float32)
        rest = lax.dot_general(both, second, nt, preferred_element_type=jnp.float32)
        return got[:8] + got[8:] + rest[:8]

    for i in range(fields):
        copies[i].wait()
        u = held_ref[0].reshape(lines, cols)
        v = held_ref[i].reshape(lines, cols)
        got = moments(v)
        flux = moments(u * v)
        at = slice(i * lines, (i + 1) * lines)
        lower_ref[0:3, at] = got[0:3]
        lower_ref[3:4, at] = flux[0:1]
        upper_ref[0:3, at] = got[3:6]
        upper_ref[3:4, at] = flux[3:4]
        head, tail = held_ref[i, :, :3], held_ref[i, :, rows - 3 :]
        inward_ref[i] = jnp.where(odd == 0, tail, head)
        outward_ref[i] = jnp.where(odd == 0, head, tail)


def mul_split(values, table):
    high, low = split(values)
    got = jnp.dot(jnp.concatenate([high, low], 1), table, preferred_element_type=jnp.float32)
    half = table.shape[1] // 2
    return got[:, :half] + got[:, half:]


def shifted(values, offset):
    planes, rows, cols = values.shape
    zeros = jnp.zeros((planes, abs(offset), cols), values.dtype)
    if offset > 0:
        return jnp.concatenate([values[:, offset:], zeros], 1)
    return jnp.concatenate([zeros, values[:, :offset]], 1)


def span_tap(v_far, w_near, w_far, distance, sign):
    odd = -0.5 * sign * span_odd[distance - 1]
    even = viscosity * span_even[distance - 1]
    return v_far * (odd * (w_near + w_far) + even)


def inner_kernel(vel_ref, old_ref, part_ref, base_ref, kept_ref, sem):
    copy = pltpu.make_async_copy(old_ref, kept_ref, sem)
    copy.start()
    planes, rows, cols = vel_ref.shape[1:]
    lines = planes * rows
    u = vel_ref[0].reshape(lines, cols)
    w = vel_ref[2]
    first = block_matrix(first_stencil, first_alpha, cols, True)
    second = block_matrix(second_stencil, second_alpha, cols, False)
    for i in range(3):
        v3 = vel_ref[i]
        v = v3.reshape(lines, cols)
        slope = mul_split(v, first)
        curve = mul_split(v, second)
        flux = mul_split(u * v, first)
        total = -0.5 * (u * slope + flux) + viscosity * curve
        total = total.reshape(planes, rows, cols) + (viscosity * span_centre) * v3
        for distance in (1, 2, 3):
            for sign in (1, -1):
                offset = sign * distance
                total = total + span_tap(shifted(v3, offset), w, shifted(w, offset), distance, sign)
        part_ref[i] = total
    copy.wait()
    for i in range(3):
        fresh = (time_step * gamma_now) * part_ref[i] + (time_step * zeta_old) * kept_ref[i]
        base_ref[i] = vel_ref[i] + fresh


def outer_kernel(
    vel_ref, left_ref, right_ref, early_out, early_in, early_part, early_base,
    late_out, late_in, late_part, late_base, new_ref, rhs_ref, new_held, rhs_held, halos, below_ref, above_ref, sems
):
    fields, planes, rows, cols = vel_ref.shape
    lines = planes * rows
    outs, ins = early_swaps(lax.axis_index("gx"))
    odd = lax.rem(lax.axis_index("gz"), 2) == 1

    def fetch(source, slot):
        return pltpu.make_async_copy(source, halos.at[slot], sems.at[slot])

    pl.when(outs)(lambda: fetch(early_out, 0).start())
    pl.when(jnp.logical_not(outs))(lambda: fetch(late_out, 0).start())
    pl.when(ins)(lambda: fetch(early_in, 1).start())
    pl.when(jnp.logical_not(ins))(lambda: fetch(late_in, 1).start())
    below_ref[...] = jnp.zeros(below_ref.shape, jnp.float32)
    above_ref[...] = jnp.zeros(above_ref.shape, jnp.float32)

    def across(part_ref, base_ref):
        u = vel_ref[0].reshape(lines, cols)
        u_edge = (left_ref[2:3, :lines], right_ref[2:3, :lines])
        table = outer_table(cols)
        tn = (((0,), (0,)), ((), ()))
        for i in range(fields):
            at = slice(i * lines, (i + 1) * lines)
            pieces = []
            for side, ref in ((0, left_ref), (1, right_ref)):
                got = ref[:, at]
                pieces += [got, got[2:3] * u_edge[side]]
            pieces.append(jnp.zeros((6, lines), jnp.float32))
            high, low = split(jnp.concatenate(pieces, 0))
            spread = lax.dot_general(
                jnp.concatenate([high, low, high], 0), table, tn, preferred_element_type=jnp.float32
            )
            extra = (spread[:, cols:] - 0.5 * u * spread[:, :cols]).reshape(planes, rows, cols)
            rhs_held[i] = part_ref[i] + extra
            new_held[i] = base_ref[i] + (time_step * gamma_now) * extra

    inner_early = jnp.logical_or(outs, ins)
    pl.when(inner_early)(lambda: across(early_part, early_base))
    pl.when(jnp.logical_not(inner_early))(lambda: across(late_part, late_base))
    fetch(early_out, 0).wait()
    fetch(early_in, 1).wait()
    below_ref[:, :, 0:3] = jnp.where(odd, halos[1], halos[0])
    above_ref[:, :, 8:11] = jnp.where(odd, halos[0], halos[1])
    w_low, w_high = vel_ref[2, :, 0:8], vel_ref[2, :, rows - 8 :]
    copies = []
    for i in range(fields):
        low_fix, high_fix = 0.0, 0.0
        for d in (1, 2, 3):
            near = slice(3 - d, 11 - d)
            low_fix = low_fix + span_tap(below_ref[i, :, near], w_low, below_ref[2, :, near], d, -1)
            near = slice(d, d + 8)
            high_fix = high_fix + span_tap(above_ref[i, :, near], w_high, above_ref[2, :, near], d, 1)
        for at, fix in ((slice(0, 8), low_fix), (slice(rows - 8, rows), high_fix)):
            rhs_held[i, :, at] += fix
            new_held[i, :, at] += (time_step * gamma_now) * fix
        for k, (source, target) in enumerate(((rhs_held, rhs_ref), (new_held, new_ref))):
            copies.append(pltpu.make_async_copy(source.at[i], target.at[i], sems.at[2 + 2 * i + k]))
            copies[-1].start()
    for copy in copies:
        copy.wait()


def send(values, axis, step):
    count = lax.axis_size(axis)
    return lax.ppermute(values, axis, [(i, (i + step) % count) for i in range(count)])


def swap(values, first, blocks):
    count = lax.axis_size("gz")
    pairs = []
    for x in blocks:
        for i in range(count // 2):
            a, b = (x * count + (2 * i + k + first) % count for k in (0, 1))
            pairs += [(a, b), (b, a)]
    return lax.ppermute(values, ("gx", "gz"), pairs)


def early_swaps(gx):
    return gx <= 1, (gx == 0) | (gx == 2)


def local(velocity, old_rhs):
    fields, planes, rows, cols = velocity.shape
    lines = planes * rows
    anywhere = pl.BlockSpec(memory_space=pl.ANY)
    whole = pl.BlockSpec(memory_space=pltpu.VMEM)
    f32 = jnp.float32
    block = pltpu.VMEM(velocity.shape, f32)
    side = pltpu.VMEM((4, fields * lines), f32)
    halo = pltpu.VMEM((fields, planes, 3, cols), f32)
    result = jax.ShapeDtypeStruct(velocity.shape, f32)
    params = pltpu.CompilerParams(vmem_limit_bytes=32 * 1024 * 1024)

    held, lower, upper, outward, inward = pl.pallas_call(
        moments_kernel,
        out_shape=(block, side, side, halo, halo),
        in_specs=[pl.BlockSpec(memory_space=pltpu.HBM)],
        out_specs=(whole,) * 5,
        scratch_shapes=[pltpu.SemaphoreType.DMA((fields,))],
        compiler_params=params,
        name="moments",
    )(pltpu.with_memory_space_constraint(velocity, pltpu.HBM))

    def inner(held, old):
        return pl.pallas_call(
            inner_kernel,
            out_shape=(block, block),
            in_specs=[whole, pl.BlockSpec(memory_space=pltpu.HBM)],
            out_specs=(whole, whole),
            scratch_shapes=[pltpu.VMEM(velocity.shape, f32), pltpu.SemaphoreType.DMA],
            compiler_params=params,
            cost_estimate=pl.CostEstimate(flops=600_000_000, bytes_accessed=1_000_000, transcendentals=0),
            name="inner",
        )(pltpu.with_memory_space_constraint(held, pltpu.VMEM), pltpu.with_memory_space_constraint(old, pltpu.HBM))

    def unset(*shapes):
        return pl.pallas_call(
            lambda *refs: None, out_shape=shapes, out_specs=(anywhere,) * len(shapes),
            compiler_params=params, name="unset",
        )()

    def after(arrays, *others):
        taken = [pltpu.with_memory_space_constraint(x, pltpu.VMEM) for x in (*arrays, *others)]
        return pl.pallas_call(
            lambda *refs: None,
            out_shape=tuple(pltpu.VMEM(x.shape, x.dtype) for x in arrays),
            in_specs=[anywhere] * len(taken),
            out_specs=(anywhere,) * len(arrays),
            input_output_aliases={i: i for i in range(len(arrays))},
            name="after",
        )(*taken)

    count = lax.axis_size("gx")
    outs, ins = early_swaps(lax.axis_index("gx"))
    kind = outs.astype(jnp.int32) + 2 * ins.astype(jnp.int32)
    chosen = [early_swaps(x) for x in range(count)]
    early_outs = [x for x in range(count) if chosen[x][0]]
    early_ins = [x for x in range(count) if chosen[x][1]]
    late_outs = [x for x in range(count) if not chosen[x][0]]
    late_ins = [x for x in range(count) if not chosen[x][1]]

    def stage(trades_out, trades_in, out_blocks, in_blocks, solves):
        def run(out, into, held, old):
            got = [swap(out, 1, out_blocks) if trades_out else None, swap(into, 0, in_blocks) if trades_in else None]
            blank = [halo] * (not trades_out) + [halo] * (not trades_in) + [block, block] * (not solves)
            solved = list(inner(held, old)) if solves else []
            blanks = list(unset(*blank)) if blank else []
            halves = [x if x is not None else blanks.pop(0) for x in got]
            return (*halves, *(solved or blanks))

        return run

    arrays = (outward, inward, held, old_rhs)
    early = lax.switch(
        kind, [stage(k in (1, 3), k in (2, 3), early_outs, early_ins, k > 0) for k in range(4)], *arrays
    )
    lower, upper = after((lower, upper), early[0], early[1])
    from_right = send(lower, "gx", -1)
    from_left = send(upper, "gx", 1)
    late = lax.switch(
        kind, [stage(k in (0, 2), k in (0, 1), late_outs, late_ins, k == 0) for k in range(4)], *arrays
    )
    scratch = pltpu.VMEM(velocity.shape, f32)
    inputs = [held, from_left, from_right, *early, *late]
    spaces = [pltpu.VMEM] * 3 + [pl.ANY, pl.ANY, pltpu.VMEM, pltpu.VMEM] * 2
    new_velocity, right_side = pl.pallas_call(
        outer_kernel,
        out_shape=(result, result),
        in_specs=[pl.BlockSpec(memory_space=x) for x in spaces],
        out_specs=(anywhere, anywhere),
        scratch_shapes=[
            scratch, scratch, pltpu.VMEM((2, *halo.shape), f32),
            *[pltpu.VMEM((fields, planes, 16, cols), f32)] * 2, pltpu.SemaphoreType.DMA((2 + 2 * fields,)),
        ],
        compiler_params=params,
        name="outer",
    )(*(pltpu.with_memory_space_constraint(x, y) for x, y in zip(inputs, spaces)))
    return new_velocity, right_side


def solution(mesh):
    spec = P(None, None, "gz", "gx")
    return jax.shard_map(local, mesh=mesh, in_specs=(spec, spec), out_specs=(spec, spec), check_vma=False)
```

```python
import functools
import math

import jax
import jax.numpy as jnp
from jax import lax
from jax.experimental import pallas as pl
from jax.experimental.pallas import tpu as pltpu
from jax.sharding import PartitionSpec as P

first_alpha = 1.0 / 3.0
first_near = 14.0 / 9.0
first_far = 1.0 / 9.0
second_alpha = 2.0 / 11.0
second_near = 12.0 / 11.0
second_far = 3.0 / 11.0
viscosity = 0.2
time_step = 0.25
gamma_now = 5.0 / 12.0
zeta_old = -17.0 / 60.0
first_stencil = (
    (1, 0.5 * first_near),
    (-1, -0.5 * first_near),
    (2, 0.25 * first_far),
    (-2, -0.25 * first_far),
)
second_stencil = (
    (0, -2.0 * second_near - 0.5 * second_far),
    (1, second_near),
    (-1, second_near),
    (2, 0.25 * second_far),
    (-2, 0.25 * second_far),
)
span_odd = (45.0 / 60.0, -9.0 / 60.0, 1.0 / 60.0)
span_even = (270.0 / 180.0, -27.0 / 180.0, 2.0 / 180.0)
span_centre = -490.0 / 180.0


def green(off_diag):
    root = (-1.0 + math.sqrt(1.0 - 4.0 * off_diag * off_diag)) / (2.0 * off_diag)
    return root, 1.0 / (1.0 + 2.0 * off_diag * root)


def weight_at(distance, stencil, off_diag):
    root, lead = green(off_diag)
    return sum(w * lead * root ** abs(distance + o) for o, w in stencil)


def reach_of(stencil, off_diag):
    root, lead = green(off_diag)
    return lead * sum(w * root**o for o, w in stencil)


def decay(away, off_diag):
    power = jnp.exp(away.astype(jnp.float32) * math.log(-green(off_diag)[0]))
    return jnp.where((away & 1) == 1, -power, power)


def block_matrix(stencil, off_diag, extent, odd):
    row = lax.broadcasted_iota(jnp.int32, (extent, extent), 0)
    column = lax.broadcasted_iota(jnp.int32, (extent, extent), 1)
    away = jnp.abs(column - row)
    far = reach_of(stencil, off_diag) * decay(away, off_diag)
    weight = jnp.where(away == 0, weight_at(0, stencil, off_diag), jnp.where(away == 1, weight_at(1, stencil, off_diag), far))
    if odd:
        weight = jnp.where(column < row, -weight, weight)
    half = jnp.concatenate(split(weight), 1)
    return jnp.concatenate([half, half], 0)


def outer_table(extent):
    row = lax.broadcasted_iota(jnp.int32, (16, 2 * extent), 0)
    column = lax.broadcasted_iota(jnp.int32, (16, 2 * extent), 1)
    left = row < 5
    kind = jnp.where(left, row, row - 5)
    slope = column < extent
    cell = jnp.where(slope, column, column - extent)
    away = jnp.where(left, cell + 1, extent - cell)
    sign = jnp.where(left, 1.0, -1.0)
    reach1, reach2 = reach_of(first_stencil, first_alpha), reach_of(second_stencil, second_alpha)
    near1 = weight_at(1, first_stencil, first_alpha) - reach1 * green(first_alpha)[0]
    near2 = weight_at(1, second_stencil, second_alpha) - reach2 * green(second_alpha)[0]
    touch = (away == 1).astype(jnp.float32)
    far1 = sign * reach1 * decay(away, first_alpha)
    far2 = viscosity * reach2 * decay(away, second_alpha)
    slopes = jnp.where(kind == 0, far1, jnp.where(kind == 2, sign * near1 * touch, 0.0))
    rests = jnp.where(kind == 1, far2, jnp.where(kind == 2, viscosity * near2 * touch, 0.0))
    rests = jnp.where(kind == 3, -0.5 * far1, jnp.where(kind == 4, -0.5 * sign * near1 * touch, rests))
    high, low = split(jnp.where(slope, slopes, rests))
    return jnp.concatenate([high, high, low], 0)


def split(values):
    high = values.astype(jnp.bfloat16)
    low = (values - high.astype(jnp.float32)).astype(jnp.bfloat16)
    return high, low


def moments_kernel(vel_ref, held_ref, first_ref, second_ref, third_ref, outward_ref, inward_ref, sems):
    fields, planes, rows, cols = vel_ref.shape
    lines = planes * rows
    copies = [
        [pltpu.make_async_copy(vel_ref.at[i, p], held_ref.at[i, p], sems.at[planes * i + p]) for p in range(planes)]
        for i in range(fields)
    ]
    for i in range(fields):
        for copy in copies[i]:
            copy.start()
    row = lax.broadcasted_iota(jnp.int32, (8, cols), 0)
    cell = lax.broadcasted_iota(jnp.int32, (8, cols), 1)
    away = jnp.where(row < 3, cell, cols - 1 - cell)
    kind = jnp.where(row < 3, row, row - 3)
    power = jnp.where(kind == 0, decay(away, first_alpha), decay(away, second_alpha))
    table = jnp.where(kind == 2, (away == 0).astype(jnp.float32), jnp.where(kind > 2, 0.0, power))
    high, low = split(table)
    both = jnp.concatenate([high, low], 0)
    gx, gz = lax.axis_index("gx"), lax.axis_index("gz")
    odd = lax.rem(gz, 2)
    first_up, second_up = upward_steps(gx, gz)
    nt = (((1,), (1,)), ((), ()))

    def moments(values):
        first, second = split(values)
        got = lax.dot_general(both, first, nt, preferred_element_type=jnp.float32)
        rest = lax.dot_general(both, second, nt, preferred_element_type=jnp.float32)
        return got[:8] + got[8:] + rest[:8]

    for i in range(fields):
        for copy in copies[i]:
            copy.wait()
        u = held_ref[0].reshape(lines, cols)
        v = held_ref[i].reshape(lines, cols)
        got = moments(v)
        flux = moments(u * v)
        at = slice(i * lines, (i + 1) * lines)
        lower = jnp.concatenate([got[0:3], flux[0:1]], 0)
        upper = jnp.concatenate([got[3:6], flux[3:4]], 0)
        first_ref[:, at] = jnp.where(first_up, upper, lower)
        second_ref[:, at] = jnp.where(second_up, upper, lower)
        third_ref[:, at] = lower
        head, tail = held_ref[i, :, :3], held_ref[i, :, rows - 3 :]
        inward_ref[i] = jnp.where(odd == 0, tail, head)
        outward_ref[i] = jnp.where(odd == 0, head, tail)


def mul_split(values, table):
    high, low = split(values)
    got = jnp.dot(jnp.concatenate([high, low], 1), table, preferred_element_type=jnp.float32)
    half = table.shape[1] // 2
    return got[:, :half] + got[:, half:]


def shifted(values, offset):
    planes, rows, cols = values.shape
    zeros = jnp.zeros((planes, abs(offset), cols), values.dtype)
    if offset > 0:
        return jnp.concatenate([values[:, offset:], zeros], 1)
    return jnp.concatenate([zeros, values[:, :offset]], 1)


def span_tap(v_far, w_near, w_far, distance, sign):
    odd = -0.5 * sign * span_odd[distance - 1]
    even = viscosity * span_even[distance - 1]
    return v_far * (odd * (w_near + w_far) + even)


def inner_kernel(vel_ref, old_ref, part_ref, base_ref, kept_ref, sem):
    copy = pltpu.make_async_copy(old_ref, kept_ref, sem)
    copy.start()
    planes, rows, cols = vel_ref.shape[1:]
    lines = planes * rows
    u = vel_ref[0].reshape(lines, cols)
    w = vel_ref[2]
    first = block_matrix(first_stencil, first_alpha, cols, True)
    second = block_matrix(second_stencil, second_alpha, cols, False)
    for i in range(3):
        v3 = vel_ref[i]
        v = v3.reshape(lines, cols)
        slope = mul_split(v, first)
        curve = mul_split(v, second)
        flux = mul_split(u * v, first)
        total = -0.5 * (u * slope + flux) + viscosity * curve
        total = total.reshape(planes, rows, cols) + (viscosity * span_centre) * v3
        for distance in (1, 2, 3):
            for sign in (1, -1):
                offset = sign * distance
                total = total + span_tap(shifted(v3, offset), w, shifted(w, offset), distance, sign)
        part_ref[i] = total
    copy.wait()
    for i in range(3):
        fresh = (time_step * gamma_now) * part_ref[i] + (time_step * zeta_old) * kept_ref[i]
        base_ref[i] = vel_ref[i] + fresh


def outer_kernel(
    vel_ref, first_ref, second_ref, third_ref, part_ref, base_ref, early_out, early_in, late_out, late_in,
    new_ref, rhs_ref, new_held, rhs_held, halos, below_ref, above_ref, sems
):
    fields, planes, rows, cols = vel_ref.shape
    lines = planes * rows
    lowest = lax.axis_index("gx") == 0
    odd = lax.rem(lax.axis_index("gz"), 2) == 1

    def fetch(source, slot):
        return pltpu.make_async_copy(source, halos.at[slot], sems.at[slot])

    @pl.when(lowest)
    def _():
        fetch(early_out, 0).start()
        fetch(early_in, 1).start()

    @pl.when(jnp.logical_not(lowest))
    def _():
        fetch(late_out, 0).start()
        fetch(late_in, 1).start()

    below_ref[...] = jnp.zeros(below_ref.shape, jnp.float32)
    above_ref[...] = jnp.zeros(above_ref.shape, jnp.float32)
    u = vel_ref[0].reshape(lines, cols)
    gx, gz = lax.axis_index("gx"), lax.axis_index("gz")
    even = lax.rem(gx, 2) == 0
    first, second, third = first_ref[...], second_ref[...], third_ref[...]
    left = jnp.where(jnp.where(gz == 0, even, gx == 1), first, second)
    right = jnp.where(gx == lax.axis_size("gx") - 1, third, jnp.where(even, second, first))
    right = jnp.where(gz == 0, right, jnp.where(gx == 0, first, third))
    u_edge = (left[2:3, :lines], right[2:3, :lines])
    table = outer_table(cols)
    tn = (((0,), (0,)), ((), ()))
    copies = []

    def across(i):
        at = slice(i * lines, (i + 1) * lines)
        pieces = []
        for side, got in ((0, left[:, at]), (1, right[:, at])):
            pieces += [got, got[2:3] * u_edge[side]]
        pieces.append(jnp.zeros((6, lines), jnp.float32))
        high, low = split(jnp.concatenate(pieces, 0))
        spread = lax.dot_general(
            jnp.concatenate([high, low, high], 0), table, tn, preferred_element_type=jnp.float32
        )
        extra = (spread[:, cols:] - 0.5 * u * spread[:, :cols]).reshape(planes, rows, cols)
        rhs_held[i] = part_ref[i] + extra
        new_held[i] = base_ref[i] + (time_step * gamma_now) * extra

    def along(i):
        w_low, w_high = vel_ref[2, :, 0:8], vel_ref[2, :, rows - 8 :]
        low_fix, high_fix = 0.0, 0.0
        for d in (1, 2, 3):
            near = slice(3 - d, 11 - d)
            low_fix = low_fix + span_tap(below_ref[i, :, near], w_low, below_ref[2, :, near], d, -1)
            near = slice(d, d + 8)
            high_fix = high_fix + span_tap(above_ref[i, :, near], w_high, above_ref[2, :, near], d, 1)
        for at, fix in ((slice(0, 8), low_fix), (slice(rows - 8, rows), high_fix)):
            rhs_held[i, :, at] += fix
            new_held[i, :, at] += (time_step * gamma_now) * fix
        for k, (source, target) in enumerate(((rhs_held, rhs_ref), (new_held, new_ref))):
            copies.append(pltpu.make_async_copy(source.at[i], target.at[i], sems.at[2 + 2 * i + k]))
            copies[-1].start()

    across(0)
    across(1)
    fetch(early_out, 0).wait()
    fetch(early_in, 1).wait()
    below_ref[:, :, 0:3] = jnp.where(odd, halos[1], halos[0])
    above_ref[:, :, 8:11] = jnp.where(odd, halos[0], halos[1])
    along(0)
    along(1)
    across(2)
    along(2)
    for copy in copies:
        copy.wait()


def upward_steps(gx, gz):
    even = lax.rem(gx, 2) == 0
    first = jnp.where(gz == 0, jnp.logical_not(even), gx == 0)
    return first, jnp.logical_or(gz > 0, even)


def step_pairs(xs, zs):
    up = lambda x, z: ((x, z), ((x + 1) % xs, z))
    down = lambda x, z: ((x, z), ((x - 1) % xs, z))
    first, second, third = [], [], []
    for z in range(1, zs):
        first += [up(0, z), down(1, z)]
        second += [up(x, z) for x in range(1, xs)]
        third += [down(x, z) for x in range(2, xs)] + [down(0, z)]
    for x in range(0, xs, 2):
        first += [up((x - 1) % xs, 0)] + [down(x, 0)] * (x > 0)
        second += [up(x, 0), down(x + 1, 0)]
    third += [down(0, 0)]
    return first, second, third


def permute(values, pairs):
    count = lax.axis_size("gz")
    return lax.ppermute(values, ("gx", "gz"), [(a * count + b, c * count + d) for (a, b), (c, d) in pairs])


def swap(values, first, blocks):
    count = lax.axis_size("gz")
    pairs = []
    for x in blocks:
        for i in range(count // 2):
            a, b = ((x, (2 * i + k + first) % count) for k in (0, 1))
            pairs += [(a, b), (b, a)]
    return permute(values, pairs)


def local(velocity, old_rhs):
    fields, planes, rows, cols = velocity.shape
    lines = planes * rows
    anywhere = pl.BlockSpec(memory_space=pl.ANY)
    whole = pl.BlockSpec(memory_space=pltpu.VMEM)
    f32 = jnp.float32
    block = pltpu.VMEM(velocity.shape, f32)
    side = pltpu.VMEM((4, fields * lines), f32)
    halo = pltpu.VMEM((fields, planes, 3, cols), f32)
    result = jax.ShapeDtypeStruct(velocity.shape, f32)
    params = pltpu.CompilerParams(vmem_limit_bytes=32 * 1024 * 1024)

    held, first, second, third, outward, inward = pl.pallas_call(
        moments_kernel,
        out_shape=(block, side, side, side, halo, halo),
        in_specs=[pl.BlockSpec(memory_space=pltpu.HBM)],
        out_specs=(whole,) * 6,
        scratch_shapes=[pltpu.SemaphoreType.DMA((fields * planes,))],
        compiler_params=params,
        name="moments",
    )(pltpu.with_memory_space_constraint(velocity, pltpu.HBM))

    def inner(held, old):
        return pl.pallas_call(
            inner_kernel,
            out_shape=(block, block),
            in_specs=[whole, pl.BlockSpec(memory_space=pltpu.HBM)],
            out_specs=(whole, whole),
            scratch_shapes=[pltpu.VMEM(velocity.shape, f32), pltpu.SemaphoreType.DMA],
            compiler_params=params,
            cost_estimate=pl.CostEstimate(flops=600_000_000, bytes_accessed=1_000_000, transcendentals=0),
            name="inner",
        )(pltpu.with_memory_space_constraint(held, pltpu.VMEM), pltpu.with_memory_space_constraint(old, pltpu.HBM))

    def unset(*shapes):
        return pl.pallas_call(
            lambda *refs: None, out_shape=shapes, out_specs=(anywhere,) * len(shapes),
            compiler_params=params, name="unset",
        )()

    def after(arrays, *others):
        taken = [pltpu.with_memory_space_constraint(x, pltpu.VMEM) for x in (*arrays, *others)]
        return pl.pallas_call(
            lambda *refs: None,
            out_shape=tuple(pltpu.VMEM(x.shape, x.dtype) for x in arrays),
            in_specs=[anywhere] * len(taken),
            out_specs=(anywhere,) * len(arrays),
            input_output_aliases={i: i for i in range(len(arrays))},
            name="after",
        )(*taken)

    xs, zs = lax.axis_size("gx"), lax.axis_size("gz")
    gx = lax.axis_index("gx")
    steps = step_pairs(xs, zs)
    rest = range(1, xs)

    def early_swaps(out, into):
        return after((swap(out, 1, [0]), swap(into, 0, [0])))

    def early_none(out, into):
        return unset(halo, halo)

    def late_none(out, into, held, old):
        return (*unset(halo, halo), *inner(held, old))

    def late_swaps(out, into, held, old):
        solved = inner(held, old)
        return (*after((swap(out, 1, rest), swap(into, 0, rest))), *solved)

    second = permute(second, steps[1])
    first = permute(first, steps[0])
    early = lax.cond(gx == 0, early_swaps, early_none, outward, inward)
    (third,) = after((third,), *early)
    third = permute(third, steps[2])
    late_out, late_in, part, base = lax.cond(gx == 0, late_none, late_swaps, outward, inward, held, old_rhs)
    scratch = pltpu.VMEM(velocity.shape, f32)
    inputs = [held, first, second, third, part, base, *early, late_out, late_in]
    spaces = [pltpu.VMEM] * 6 + [pl.ANY] * 4
    new_velocity, right_side = pl.pallas_call(
        outer_kernel,
        out_shape=(result, result),
        in_specs=[pl.BlockSpec(memory_space=x) for x in spaces],
        out_specs=(anywhere, anywhere),
        scratch_shapes=[
            scratch, scratch, pltpu.VMEM((2, *halo.shape), f32),
            *[pltpu.VMEM((fields, planes, 16, cols), f32)] * 2, pltpu.SemaphoreType.DMA((2 + 2 * fields,)),
        ],
        compiler_params=params,
        name="outer",
    )(*(pltpu.with_memory_space_constraint(x, y) for x, y in zip(inputs, spaces)))
    return new_velocity, right_side


def solution(mesh):
    spec = P(None, None, "gz", "gx")
    return jax.shard_map(local, mesh=mesh, in_specs=(spec, spec), out_specs=(spec, spec), check_vma=False)
```

```python
import functools
import math

import jax
import jax.numpy as jnp
from jax import lax
from jax.experimental import pallas as pl
from jax.experimental.pallas import tpu as pltpu
from jax.sharding import PartitionSpec as P

first_alpha = 1.0 / 3.0
first_near = 14.0 / 9.0
first_far = 1.0 / 9.0
second_alpha = 2.0 / 11.0
second_near = 12.0 / 11.0
second_far = 3.0 / 11.0
viscosity = 0.2
time_step = 0.25
gamma_now = 5.0 / 12.0
zeta_old = -17.0 / 60.0
first_stencil = (
    (1, 0.5 * first_near),
    (-1, -0.5 * first_near),
    (2, 0.25 * first_far),
    (-2, -0.25 * first_far),
)
second_stencil = (
    (0, -2.0 * second_near - 0.5 * second_far),
    (1, second_near),
    (-1, second_near),
    (2, 0.25 * second_far),
    (-2, 0.25 * second_far),
)
span_odd = (45.0 / 60.0, -9.0 / 60.0, 1.0 / 60.0)
span_even = (270.0 / 180.0, -27.0 / 180.0, 2.0 / 180.0)
span_centre = -490.0 / 180.0


def green(off_diag):
    root = (-1.0 + math.sqrt(1.0 - 4.0 * off_diag * off_diag)) / (2.0 * off_diag)
    return root, 1.0 / (1.0 + 2.0 * off_diag * root)


def weight_at(distance, stencil, off_diag):
    root, lead = green(off_diag)
    return sum(w * lead * root ** abs(distance + o) for o, w in stencil)


def reach_of(stencil, off_diag):
    root, lead = green(off_diag)
    return lead * sum(w * root**o for o, w in stencil)


def decay(away, off_diag):
    power = jnp.exp(away.astype(jnp.float32) * math.log(-green(off_diag)[0]))
    return jnp.where((away & 1) == 1, -power, power)


def block_matrix(stencil, off_diag, extent, odd):
    row = lax.broadcasted_iota(jnp.int32, (extent, extent), 0)
    column = lax.broadcasted_iota(jnp.int32, (extent, extent), 1)
    away = jnp.abs(column - row)
    far = reach_of(stencil, off_diag) * decay(away, off_diag)
    weight = jnp.where(away == 0, weight_at(0, stencil, off_diag), jnp.where(away == 1, weight_at(1, stencil, off_diag), far))
    if odd:
        weight = jnp.where(column < row, -weight, weight)
    half = jnp.concatenate(split(weight), 1)
    return jnp.concatenate([half, half], 0)


def outer_table(extent):
    row = lax.broadcasted_iota(jnp.int32, (16, 2 * extent), 0)
    column = lax.broadcasted_iota(jnp.int32, (16, 2 * extent), 1)
    left = row < 5
    kind = jnp.where(left, row, row - 5)
    slope = column < extent
    cell = jnp.where(slope, column, column - extent)
    away = jnp.where(left, cell + 1, extent - cell)
    sign = jnp.where(left, 1.0, -1.0)
    reach1, reach2 = reach_of(first_stencil, first_alpha), reach_of(second_stencil, second_alpha)
    near1 = weight_at(1, first_stencil, first_alpha) - reach1 * green(first_alpha)[0]
    near2 = weight_at(1, second_stencil, second_alpha) - reach2 * green(second_alpha)[0]
    touch = (away == 1).astype(jnp.float32)
    far1 = sign * reach1 * decay(away, first_alpha)
    far2 = viscosity * reach2 * decay(away, second_alpha)
    slopes = jnp.where(kind == 0, far1, jnp.where(kind == 2, sign * near1 * touch, 0.0))
    rests = jnp.where(kind == 1, far2, jnp.where(kind == 2, viscosity * near2 * touch, 0.0))
    rests = jnp.where(kind == 3, -0.5 * far1, jnp.where(kind == 4, -0.5 * sign * near1 * touch, rests))
    high, low = split(jnp.where(slope, slopes, rests))
    return jnp.concatenate([high, high, low], 0)


def split(values):
    high = values.astype(jnp.bfloat16)
    low = (values - high.astype(jnp.float32)).astype(jnp.bfloat16)
    return high, low


def moments_kernel(vel_ref, held_ref, first_ref, second_ref, third_ref, outward_ref, inward_ref, sems):
    fields, planes, rows, cols = vel_ref.shape
    lines = planes * rows
    copies = [
        [pltpu.make_async_copy(vel_ref.at[i, p], held_ref.at[i, p], sems.at[planes * i + p]) for p in range(planes)]
        for i in range(fields)
    ]
    for i in range(fields):
        for copy in copies[i]:
            copy.start()
    row = lax.broadcasted_iota(jnp.int32, (8, cols), 0)
    cell = lax.broadcasted_iota(jnp.int32, (8, cols), 1)
    away = jnp.where(row < 3, cell, cols - 1 - cell)
    kind = jnp.where(row < 3, row, row - 3)
    power = jnp.where(kind == 0, decay(away, first_alpha), decay(away, second_alpha))
    table = jnp.where(kind == 2, (away == 0).astype(jnp.float32), jnp.where(kind > 2, 0.0, power))
    high, low = split(table)
    both = jnp.concatenate([high, low], 0)
    gx, gz = lax.axis_index("gx"), lax.axis_index("gz")
    odd = lax.rem(gz, 2)
    first_up, second_up = upward_steps(gx, gz)
    nt = (((1,), (1,)), ((), ()))

    def moments(values):
        first, second = split(values)
        got = lax.dot_general(both, first, nt, preferred_element_type=jnp.float32)
        rest = lax.dot_general(both, second, nt, preferred_element_type=jnp.float32)
        return got[:8] + got[8:] + rest[:8]

    for i in range(fields):
        for copy in copies[i]:
            copy.wait()
        u = held_ref[0].reshape(lines, cols)
        v = held_ref[i].reshape(lines, cols)
        got = moments(v)
        flux = moments(u * v)
        at = slice(i * lines, (i + 1) * lines)
        lower = jnp.concatenate([got[0:3], flux[0:1]], 0)
        upper = jnp.concatenate([got[3:6], flux[3:4]], 0)
        first_ref[:, at] = jnp.where(first_up, upper, lower)
        second_ref[:, at] = jnp.where(second_up, upper, lower)
        third_ref[:, at] = lower
        head, tail = held_ref[i, :, :3], held_ref[i, :, rows - 3 :]
        inward_ref[i] = jnp.where(odd == 0, tail, head)
        outward_ref[i] = jnp.where(odd == 0, head, tail)


def mul_split(values, table):
    high, low = split(values)
    got = jnp.dot(jnp.concatenate([high, low], 1), table, preferred_element_type=jnp.float32)
    half = table.shape[1] // 2
    return got[:, :half] + got[:, half:]


def shifted(values, offset):
    planes, rows, cols = values.shape
    zeros = jnp.zeros((planes, abs(offset), cols), values.dtype)
    if offset > 0:
        return jnp.concatenate([values[:, offset:], zeros], 1)
    return jnp.concatenate([zeros, values[:, :offset]], 1)


def span_tap(v_far, w_near, w_far, distance, sign):
    odd = -0.5 * sign * span_odd[distance - 1]
    even = viscosity * span_even[distance - 1]
    return v_far * (odd * (w_near + w_far) + even)


def lowest_kernel(vel_ref, old_ref, early_out, early_in, part_ref, base_ref, outward_ref, inward_ref, kept_ref, sem, sems):
    moves = [
        pltpu.make_async_copy(early_out, outward_ref, sems.at[0]),
        pltpu.make_async_copy(early_in, inward_ref, sems.at[1]),
    ]
    for move in moves:
        move.start()
    inner_kernel(vel_ref, old_ref, part_ref, base_ref, kept_ref, sem)
    for move in moves:
        move.wait()


def inner_kernel(vel_ref, old_ref, part_ref, base_ref, kept_ref, sem):
    copy = pltpu.make_async_copy(old_ref, kept_ref, sem)
    copy.start()
    planes, rows, cols = vel_ref.shape[1:]
    lines = planes * rows
    u = vel_ref[0].reshape(lines, cols)
    w = vel_ref[2]
    first = block_matrix(first_stencil, first_alpha, cols, True)
    second = block_matrix(second_stencil, second_alpha, cols, False)
    for i in range(3):
        v3 = vel_ref[i]
        v = v3.reshape(lines, cols)
        slope = mul_split(v, first)
        curve = mul_split(v, second)
        flux = mul_split(u * v, first)
        total = -0.5 * (u * slope + flux) + viscosity * curve
        total = total.reshape(planes, rows, cols) + (viscosity * span_centre) * v3
        for distance in (1, 2, 3):
            for sign in (1, -1):
                offset = sign * distance
                total = total + span_tap(shifted(v3, offset), w, shifted(w, offset), distance, sign)
        part_ref[i] = total
    copy.wait()
    for i in range(3):
        fresh = (time_step * gamma_now) * part_ref[i] + (time_step * zeta_old) * kept_ref[i]
        base_ref[i] = vel_ref[i] + fresh


def outer_kernel(
    vel_ref, first_ref, second_ref, third_ref, part_ref, base_ref, outward_ref, inward_ref, early_out, early_in,
    new_ref, rhs_ref, new_held, rhs_held, below_ref, above_ref, sems
):
    fields, planes, rows, cols = vel_ref.shape
    lines = planes * rows
    below_ref[...] = jnp.zeros(below_ref.shape, jnp.float32)
    above_ref[...] = jnp.zeros(above_ref.shape, jnp.float32)
    odd = lax.rem(lax.axis_index("gz"), 2) == 1
    below_ref[:, :, 0:3] = jnp.where(odd, inward_ref[...], outward_ref[...])
    above_ref[:, :, 8:11] = jnp.where(odd, outward_ref[...], inward_ref[...])
    u = vel_ref[0].reshape(lines, cols)
    gx, gz = lax.axis_index("gx"), lax.axis_index("gz")
    left, right = arrivals(gx, gz, first_ref[...], second_ref[...], third_ref[...])
    u_edge = (left[2:3, :lines], right[2:3, :lines])
    table = outer_table(cols)
    tn = (((0,), (0,)), ((), ()))
    copies = []

    def across(i):
        at = slice(i * lines, (i + 1) * lines)
        pieces = []
        for side, got in ((0, left[:, at]), (1, right[:, at])):
            pieces += [got, got[2:3] * u_edge[side]]
        pieces.append(jnp.zeros((6, lines), jnp.float32))
        high, low = split(jnp.concatenate(pieces, 0))
        spread = lax.dot_general(
            jnp.concatenate([high, low, high], 0), table, tn, preferred_element_type=jnp.float32
        )
        extra = (spread[:, cols:] - 0.5 * u * spread[:, :cols]).reshape(planes, rows, cols)
        rhs_held[i] = part_ref[i] + extra
        new_held[i] = base_ref[i] + (time_step * gamma_now) * extra

    def along(i):
        w_low, w_high = vel_ref[2, :, 0:8], vel_ref[2, :, rows - 8 :]
        low_fix, high_fix = 0.0, 0.0
        for d in (1, 2, 3):
            near = slice(3 - d, 11 - d)
            low_fix = low_fix + span_tap(below_ref[i, :, near], w_low, below_ref[2, :, near], d, -1)
            near = slice(d, d + 8)
            high_fix = high_fix + span_tap(above_ref[i, :, near], w_high, above_ref[2, :, near], d, 1)
        for at, fix in ((slice(0, 8), low_fix), (slice(rows - 8, rows), high_fix)):
            rhs_held[i, :, at] += fix
            new_held[i, :, at] += (time_step * gamma_now) * fix
        for k, (source, target) in enumerate(((rhs_held, rhs_ref), (new_held, new_ref))):
            copies.append(pltpu.make_async_copy(source.at[i], target.at[i], sems.at[2 * i + k]))
            copies[-1].start()

    for i in range(fields):
        across(i)
        along(i)
    for copy in copies:
        copy.wait()


def upward_steps(gx, gz):
    last = lax.axis_size("gx") - 1
    first = jnp.where(gz == 0, jnp.logical_or(gx == 1, gx == last), gx == 0)
    return first, jnp.logical_or(gz > 0, gx != 1)


def step_pairs(xs, zs):
    up = lambda x, z: ((x, z), ((x + 1) % xs, z))
    down = lambda x, z: ((x, z), ((x - 1) % xs, z))
    first = [up(1, 0), down(2, 0), up(xs - 1, 0)] + [down(x, 0) for x in range(4, xs - 1)]
    second = [up(0, 0), down(1, 0)] + [up(x, 0) for x in range(2, xs - 1)]
    third = [down(3, 0), down(xs - 1, 0), down(0, 0)]
    for z in range(1, zs):
        first += [up(0, z), down(1, z)]
        second += [up(x, z) for x in range(1, xs)]
        third += [down(x, z) for x in range(2, xs)] + [down(0, z)]
    return first, second, third


def arrivals(gx, gz, first, second, third):
    last = lax.axis_size("gx") - 1
    left = jnp.where(jnp.where(gz == 0, jnp.logical_or(gx == 0, gx == 2), gx == 1), first, second)
    late = jnp.logical_or(gx == 2, gx >= last - 1)
    column = jnp.where(gx == 0, second, jnp.where(late, third, first))
    return left, jnp.where(gz == 0, column, jnp.where(gx == 0, first, third))


def permute(values, pairs):
    count = lax.axis_size("gz")
    return lax.ppermute(values, ("gx", "gz"), [(a * count + b, c * count + d) for (a, b), (c, d) in pairs])


def swap(values, first, blocks):
    count = lax.axis_size("gz")
    pairs = []
    for x in blocks:
        for i in range(count // 2):
            a, b = ((x, (2 * i + k + first) % count) for k in (0, 1))
            pairs += [(a, b), (b, a)]
    return permute(values, pairs)


def local(velocity, old_rhs):
    fields, planes, rows, cols = velocity.shape
    lines = planes * rows
    anywhere = pl.BlockSpec(memory_space=pl.ANY)
    whole = pl.BlockSpec(memory_space=pltpu.VMEM)
    f32 = jnp.float32
    block = pltpu.VMEM(velocity.shape, f32)
    side = pltpu.VMEM((4, fields * lines), f32)
    halo = pltpu.VMEM((fields, planes, 3, cols), f32)
    result = jax.ShapeDtypeStruct(velocity.shape, f32)
    params = pltpu.CompilerParams(vmem_limit_bytes=32 * 1024 * 1024)

    held, first, second, third, outward, inward = pl.pallas_call(
        moments_kernel,
        out_shape=(block, side, side, side, halo, halo),
        in_specs=[pl.BlockSpec(memory_space=pltpu.HBM)],
        out_specs=(whole,) * 6,
        scratch_shapes=[pltpu.SemaphoreType.DMA((fields * planes,))],
        compiler_params=params,
        name="moments",
    )(pltpu.with_memory_space_constraint(velocity, pltpu.HBM))

    def inner(held, old, *more):
        spaces = [pltpu.VMEM, pltpu.HBM] + [pl.ANY] * len(more)
        return pl.pallas_call(
            lowest_kernel if more else inner_kernel,
            out_shape=(block, block) + (halo,) * len(more),
            in_specs=[pl.BlockSpec(memory_space=x) for x in spaces],
            out_specs=(whole,) * (2 + len(more)),
            scratch_shapes=[pltpu.VMEM(velocity.shape, f32), pltpu.SemaphoreType.DMA]
            + [pltpu.SemaphoreType.DMA((2,))] * bool(more),
            compiler_params=params,
            cost_estimate=pl.CostEstimate(flops=600_000_000, bytes_accessed=1_000_000, transcendentals=0),
            name="inner",
        )(*(pltpu.with_memory_space_constraint(x, y) for x, y in zip((held, old, *more), spaces)))

    def unset(*shapes):
        return pl.pallas_call(
            lambda *refs: None, out_shape=shapes, out_specs=(anywhere,) * len(shapes),
            compiler_params=params, name="unset",
        )()

    def after(arrays, *others):
        taken = [pltpu.with_memory_space_constraint(x, pltpu.VMEM) for x in (*arrays, *others)]
        return pl.pallas_call(
            lambda *refs: None,
            out_shape=tuple(pltpu.VMEM(x.shape, x.dtype) for x in arrays),
            in_specs=[anywhere] * len(taken),
            out_specs=(anywhere,) * len(arrays),
            input_output_aliases={i: i for i in range(len(arrays))},
            name="after",
        )(*taken)

    xs, zs = lax.axis_size("gx"), lax.axis_size("gz")
    gx = lax.axis_index("gx")
    steps = step_pairs(xs, zs)
    rest = range(1, xs)

    def early_swaps(out, into):
        return after((swap(out, 1, [0]), swap(into, 0, [0])))

    def early_none(out, into):
        return unset(halo, halo)

    def late_none(out, into, early_out, early_in, held, old):
        part, base, out, into = inner(held, old, early_out, early_in)
        return out, into, part, base

    def late_swaps(out, into, early_out, early_in, held, old):
        part, base = inner(held, old)
        return (*after((swap(out, 1, rest), swap(into, 0, rest))), part, base)

    second = permute(second, steps[1])
    first = permute(first, steps[0])
    early = lax.cond(gx == 0, early_swaps, early_none, outward, inward)
    (third,) = after((third,), *early)
    third = permute(third, steps[2])
    out, into, part, base = lax.cond(gx == 0, late_none, late_swaps, outward, inward, *early, held, old_rhs)
    scratch = pltpu.VMEM(velocity.shape, f32)
    new_velocity, right_side = pl.pallas_call(
        outer_kernel,
        out_shape=(result, result),
        in_specs=[whole] * 8 + [anywhere] * 2,
        out_specs=(anywhere, anywhere),
        scratch_shapes=[
            scratch, scratch, *[pltpu.VMEM((fields, planes, 16, cols), f32)] * 2,
            pltpu.SemaphoreType.DMA((2 * fields,)),
        ],
        compiler_params=params,
        name="outer",
    )(*(pltpu.with_memory_space_constraint(x, pltpu.VMEM) for x in (held, first, second, third, part, base, out, into)), *early)
    return new_velocity, right_side


def solution(mesh):
    spec = P(None, None, "gz", "gx")
    return jax.shard_map(local, mesh=mesh, in_specs=(spec, spec), out_specs=(spec, spec), check_vma=False)
```

```python
import functools
import math

import jax
import jax.numpy as jnp
from jax import lax
from jax.experimental import pallas as pl
from jax.experimental.pallas import tpu as pltpu
from jax.sharding import PartitionSpec as P

first_alpha = 1.0 / 3.0
first_near = 14.0 / 9.0
first_far = 1.0 / 9.0
second_alpha = 2.0 / 11.0
second_near = 12.0 / 11.0
second_far = 3.0 / 11.0
viscosity = 0.2
time_step = 0.25
gamma_now = 5.0 / 12.0
zeta_old = -17.0 / 60.0
first_stencil = (
    (1, 0.5 * first_near),
    (-1, -0.5 * first_near),
    (2, 0.25 * first_far),
    (-2, -0.25 * first_far),
)
second_stencil = (
    (0, -2.0 * second_near - 0.5 * second_far),
    (1, second_near),
    (-1, second_near),
    (2, 0.25 * second_far),
    (-2, 0.25 * second_far),
)
span_odd = (45.0 / 60.0, -9.0 / 60.0, 1.0 / 60.0)
span_even = (270.0 / 180.0, -27.0 / 180.0, 2.0 / 180.0)
span_centre = -490.0 / 180.0


def green(off_diag):
    root = (-1.0 + math.sqrt(1.0 - 4.0 * off_diag * off_diag)) / (2.0 * off_diag)
    return root, 1.0 / (1.0 + 2.0 * off_diag * root)


def weight_at(distance, stencil, off_diag):
    root, lead = green(off_diag)
    return sum(w * lead * root ** abs(distance + o) for o, w in stencil)


def reach_of(stencil, off_diag):
    root, lead = green(off_diag)
    return lead * sum(w * root**o for o, w in stencil)


def decay(away, off_diag):
    power = jnp.exp(away.astype(jnp.float32) * math.log(-green(off_diag)[0]))
    return jnp.where((away & 1) == 1, -power, power)


def block_matrix(stencil, off_diag, extent, odd):
    row = lax.broadcasted_iota(jnp.int32, (extent, extent), 0)
    column = lax.broadcasted_iota(jnp.int32, (extent, extent), 1)
    away = jnp.abs(column - row)
    far = reach_of(stencil, off_diag) * decay(away, off_diag)
    weight = jnp.where(away == 0, weight_at(0, stencil, off_diag), jnp.where(away == 1, weight_at(1, stencil, off_diag), far))
    if odd:
        weight = jnp.where(column < row, -weight, weight)
    half = jnp.concatenate(split(weight), 1)
    return jnp.concatenate([half, half], 0)


def outer_table(extent):
    row = lax.broadcasted_iota(jnp.int32, (16, 2 * extent), 0)
    column = lax.broadcasted_iota(jnp.int32, (16, 2 * extent), 1)
    left = row < 5
    kind = jnp.where(left, row, row - 5)
    slope = column < extent
    cell = jnp.where(slope, column, column - extent)
    away = jnp.where(left, cell + 1, extent - cell)
    sign = jnp.where(left, 1.0, -1.0)
    reach1, reach2 = reach_of(first_stencil, first_alpha), reach_of(second_stencil, second_alpha)
    near1 = weight_at(1, first_stencil, first_alpha) - reach1 * green(first_alpha)[0]
    near2 = weight_at(1, second_stencil, second_alpha) - reach2 * green(second_alpha)[0]
    touch = (away == 1).astype(jnp.float32)
    far1 = sign * reach1 * decay(away, first_alpha)
    far2 = viscosity * reach2 * decay(away, second_alpha)
    slopes = jnp.where(kind == 0, far1, jnp.where(kind == 2, sign * near1 * touch, 0.0))
    rests = jnp.where(kind == 1, far2, jnp.where(kind == 2, viscosity * near2 * touch, 0.0))
    rests = jnp.where(kind == 3, -0.5 * far1, jnp.where(kind == 4, -0.5 * sign * near1 * touch, rests))
    high, low = split(jnp.where(slope, slopes, rests))
    return jnp.concatenate([high, high, low], 0)


def split(values):
    high = values.astype(jnp.bfloat16)
    low = (values - high.astype(jnp.float32)).astype(jnp.bfloat16)
    return high, low


def moments_kernel(vel_ref, held_ref, first_ref, second_ref, third_ref, outward_ref, inward_ref, sems):
    fields, planes, rows, cols = vel_ref.shape
    lines = planes * rows
    copies = [
        [pltpu.make_async_copy(vel_ref.at[i, p], held_ref.at[i, p], sems.at[planes * i + p]) for p in range(planes)]
        for i in range(fields)
    ]
    for i in range(fields):
        for copy in copies[i]:
            copy.start()
    row = lax.broadcasted_iota(jnp.int32, (8, cols), 0)
    cell = lax.broadcasted_iota(jnp.int32, (8, cols), 1)
    away = jnp.where(row < 3, cell, cols - 1 - cell)
    kind = jnp.where(row < 3, row, row - 3)
    power = jnp.where(kind == 0, decay(away, first_alpha), decay(away, second_alpha))
    table = jnp.where(kind == 2, (away == 0).astype(jnp.float32), jnp.where(kind > 2, 0.0, power))
    high, low = split(table)
    both = jnp.concatenate([high, low], 0)
    gx, gz = lax.axis_index("gx"), lax.axis_index("gz")
    odd = lax.rem(gz, 2)
    first_up, second_up = upward_steps(gx, gz)
    nt = (((1,), (1,)), ((), ()))

    for i in range(fields):
        for copy in copies[i]:
            copy.wait()
    u = held_ref[0].reshape(lines, cols)
    v = held_ref[...].reshape(fields * lines, cols)
    terms = [v] + [u * held_ref[i].reshape(lines, cols) for i in range(fields)]
    near, rest = split(jnp.concatenate(terms, 0))
    all_got = lax.dot_general(both, near, nt, preferred_element_type=jnp.float32)
    rest_got = lax.dot_general(high, rest, nt, preferred_element_type=jnp.float32)
    all_got = all_got[:8] + all_got[8:] + rest_got
    for i in range(fields):
        got = all_got[:, i * lines : (i + 1) * lines]
        flux = all_got[:, (fields + i) * lines : (fields + i + 1) * lines]
        at = slice(i * lines, (i + 1) * lines)
        lower = jnp.concatenate([got[0:3], flux[0:1]], 0)
        upper = jnp.concatenate([got[3:6], flux[3:4]], 0)
        first_ref[:, at] = jnp.where(first_up, upper, lower)
        second_ref[:, at] = jnp.where(second_up, upper, lower)
        third_ref[:, at] = lower
        head, tail = held_ref[i, :, :3], held_ref[i, :, rows - 3 :]
        inward_ref[i] = jnp.where(odd == 0, tail, head)
        outward_ref[i] = jnp.where(odd == 0, head, tail)


def mul_split(values, table):
    high, low = split(values)
    got = jnp.dot(jnp.concatenate([high, low], 1), table, preferred_element_type=jnp.float32)
    half = table.shape[1] // 2
    return got[:, :half] + got[:, half:]


def shifted(values, offset):
    planes, rows, cols = values.shape
    zeros = jnp.zeros((planes, abs(offset), cols), values.dtype)
    if offset > 0:
        return jnp.concatenate([values[:, offset:], zeros], 1)
    return jnp.concatenate([zeros, values[:, :offset]], 1)


def span_tap(v_far, w_near, w_far, distance, sign):
    odd = -0.5 * sign * span_odd[distance - 1]
    even = viscosity * span_even[distance - 1]
    return v_far * (odd * (w_near + w_far) + even)


def inner_kernel(vel_ref, old_ref, part_ref, base_ref, kept_ref, sem):
    copy = pltpu.make_async_copy(old_ref, kept_ref, sem)
    copy.start()
    planes, rows, cols = vel_ref.shape[1:]
    lines = planes * rows
    u = vel_ref[0].reshape(lines, cols)
    w = vel_ref[2]
    first = block_matrix(first_stencil, first_alpha, cols, True)
    second = block_matrix(second_stencil, second_alpha, cols, False)
    for i in range(3):
        v3 = vel_ref[i]
        v = v3.reshape(lines, cols)
        slope = mul_split(v, first)
        curve = mul_split(v, second)
        flux = mul_split(u * v, first)
        total = -0.5 * (u * slope + flux) + viscosity * curve
        total = total.reshape(planes, rows, cols) + (viscosity * span_centre) * v3
        for distance in (1, 2, 3):
            for sign in (1, -1):
                offset = sign * distance
                total = total + span_tap(shifted(v3, offset), w, shifted(w, offset), distance, sign)
        part_ref[i] = total
    copy.wait()
    for i in range(3):
        fresh = (time_step * gamma_now) * part_ref[i] + (time_step * zeta_old) * kept_ref[i]
        base_ref[i] = vel_ref[i] + fresh


def set_margins(outward, inward, below_ref, above_ref):
    odd = lax.rem(lax.axis_index("gz"), 2) == 1
    below_ref[...] = jnp.zeros(below_ref.shape, jnp.float32)
    above_ref[...] = jnp.zeros(above_ref.shape, jnp.float32)
    below_ref[:, :, 0:3] = jnp.where(odd, inward, outward)
    above_ref[:, :, 8:11] = jnp.where(odd, outward, inward)


def edge_terms(vel_ref, below_ref, above_ref, i):
    rows = vel_ref.shape[2]
    w_low, w_high = vel_ref[2, :, 0:8], vel_ref[2, :, rows - 8 :]
    low, high = 0.0, 0.0
    for d in (1, 2, 3):
        near = slice(3 - d, 11 - d)
        low = low + span_tap(below_ref[i, :, near], w_low, below_ref[2, :, near], d, -1)
        near = slice(d, d + 8)
        high = high + span_tap(above_ref[i, :, near], w_high, above_ref[2, :, near], d, 1)
    return low, high


def edges_kernel(vel_ref, outward_ref, inward_ref, edges_ref, below_ref, above_ref):
    set_margins(outward_ref[...], inward_ref[...], below_ref, above_ref)
    for i in range(vel_ref.shape[0]):
        edges_ref[i, :, 0:8], edges_ref[i, :, 8:16] = edge_terms(vel_ref, below_ref, above_ref, i)


def lowest_kernel(
    vel_ref, first_ref, second_ref, part_ref, base_ref, edges_ref, late_ref,
    new_ref, rhs_ref, new_held, rhs_held, sems
):
    @pl.when(lax.axis_index("gx") == 0)
    def _():
        finish(
            vel_ref, first_ref, second_ref, None, part_ref, base_ref,
            lambda i: (edges_ref[i, :, 0:8], edges_ref[i, :, 8:16]),
            new_ref, rhs_ref, new_held, rhs_held, sems
        )


def outer_kernel(
    vel_ref, first_ref, second_ref, third_ref, part_ref, base_ref, outward_ref, inward_ref, new_before, rhs_before,
    new_ref, rhs_ref, new_held, rhs_held, below_ref, above_ref, sems
):
    @pl.when(lax.axis_index("gx") > 0)
    def _():
        set_margins(outward_ref[...], inward_ref[...], below_ref, above_ref)
        finish(
            vel_ref, first_ref, second_ref, third_ref, part_ref, base_ref,
            functools.partial(edge_terms, vel_ref, below_ref, above_ref),
            new_ref, rhs_ref, new_held, rhs_held, sems
        )


def finish(
    vel_ref, first_ref, second_ref, third_ref, part_ref, base_ref, edges,
    new_ref, rhs_ref, new_held, rhs_held, sems
):
    fields, planes, rows, cols = vel_ref.shape
    lines = planes * rows
    u = vel_ref[0].reshape(lines, cols)
    gx, gz = lax.axis_index("gx"), lax.axis_index("gz")
    left, right = arrivals(gx, gz, first_ref[...], second_ref[...], None if third_ref is None else third_ref[...])
    u_edge = (left[2:3, :lines], right[2:3, :lines])
    table = outer_table(cols)
    tn = (((0,), (0,)), ((), ()))
    copies = []

    def across(i):
        at = slice(i * lines, (i + 1) * lines)
        pieces = []
        for side, got in ((0, left[:, at]), (1, right[:, at])):
            pieces += [got, got[2:3] * u_edge[side]]
        pieces.append(jnp.zeros((6, lines), jnp.float32))
        high, low = split(jnp.concatenate(pieces, 0))
        spread = lax.dot_general(
            jnp.concatenate([high, low, high], 0), table, tn, preferred_element_type=jnp.float32
        )
        extra = (spread[:, cols:] - 0.5 * u * spread[:, :cols]).reshape(planes, rows, cols)
        rhs_held[i] = part_ref[i] + extra
        new_held[i] = base_ref[i] + (time_step * gamma_now) * extra

    def along(i):
        low_fix, high_fix = edges(i)
        for at, fix in ((slice(0, 8), low_fix), (slice(rows - 8, rows), high_fix)):
            rhs_held[i, :, at] += fix
            new_held[i, :, at] += (time_step * gamma_now) * fix
        for k, (source, target) in enumerate(((rhs_held, rhs_ref), (new_held, new_ref))):
            copies.append(pltpu.make_async_copy(source.at[i], target.at[i], sems.at[2 * i + k]))
            copies[-1].start()

    for i in range(fields):
        across(i)
        along(i)
    for copy in copies:
        copy.wait()


def upward_steps(gx, gz):
    last = lax.axis_size("gx") - 1
    first = jnp.where(gz == 0, jnp.logical_or(gx == 1, gx == last), gx == 0)
    return first, jnp.logical_or(gz > 0, gx != 1)


def step_pairs(xs, zs):
    up = lambda x, z: ((x, z), ((x + 1) % xs, z))
    down = lambda x, z: ((x, z), ((x - 1) % xs, z))
    first = [up(1, 0), down(2, 0), up(xs - 1, 0)] + [down(x, 0) for x in range(4, xs - 1)]
    second = [up(0, 0), down(1, 0)] + [up(x, 0) for x in range(2, xs - 1)]
    third = [down(3, 0), down(xs - 1, 0), down(0, 0)]
    for z in range(1, zs):
        first += [up(0, z), down(1, z)]
        second += [up(x, z) for x in range(1, xs)]
        third += [down(x, z) for x in range(2, xs)] + [down(0, z)]
    return first, second, third


def arrivals(gx, gz, first, second, third):
    last = lax.axis_size("gx") - 1
    left = jnp.where(jnp.where(gz == 0, jnp.logical_or(gx == 0, gx == 2), gx == 1), first, second)
    if third is None:
        return left, jnp.where(gz == 0, second, first)
    late = jnp.logical_or(gx == 2, gx >= last - 1)
    column = jnp.where(gx == 0, second, jnp.where(late, third, first))
    return left, jnp.where(gz == 0, column, jnp.where(gx == 0, first, third))


def permute(values, pairs):
    count = lax.axis_size("gz")
    return lax.ppermute(values, ("gx", "gz"), [(a * count + b, c * count + d) for (a, b), (c, d) in pairs])


def swap(values, first, blocks):
    count = lax.axis_size("gz")
    pairs = []
    for x in blocks:
        for i in range(count // 2):
            a, b = ((x, (2 * i + k + first) % count) for k in (0, 1))
            pairs += [(a, b), (b, a)]
    return permute(values, pairs)


def local(velocity, old_rhs):
    fields, planes, rows, cols = velocity.shape
    lines = planes * rows
    anywhere = pl.BlockSpec(memory_space=pl.ANY)
    whole = pl.BlockSpec(memory_space=pltpu.VMEM)
    f32 = jnp.float32
    block = pltpu.VMEM(velocity.shape, f32)
    side = pltpu.VMEM((4, fields * lines), f32)
    halo = pltpu.VMEM((fields, planes, 3, cols), f32)
    edge = pltpu.VMEM((fields, planes, 16, cols), f32)
    margins = edge
    result = jax.ShapeDtypeStruct(velocity.shape, f32)
    params = pltpu.CompilerParams(vmem_limit_bytes=32 * 1024 * 1024)

    held, first, second, third, outward, inward = pl.pallas_call(
        moments_kernel,
        out_shape=(block, side, side, side, halo, halo),
        in_specs=[pl.BlockSpec(memory_space=pltpu.HBM)],
        out_specs=(whole,) * 6,
        scratch_shapes=[pltpu.SemaphoreType.DMA((fields * planes,))],
        compiler_params=params,
        name="moments",
    )(pltpu.with_memory_space_constraint(velocity, pltpu.HBM))

    def inner(held, old):
        return pl.pallas_call(
            inner_kernel,
            out_shape=(block, block),
            in_specs=[whole, pl.BlockSpec(memory_space=pltpu.HBM)],
            out_specs=(whole, whole),
            scratch_shapes=[pltpu.VMEM(velocity.shape, f32), pltpu.SemaphoreType.DMA],
            compiler_params=params,
            cost_estimate=pl.CostEstimate(flops=600_000_000, bytes_accessed=1_000_000, transcendentals=0),
            name="inner",
        )(pltpu.with_memory_space_constraint(held, pltpu.VMEM), pltpu.with_memory_space_constraint(old, pltpu.HBM))

    def unset(*shapes):
        return pl.pallas_call(
            lambda *refs: None, out_shape=shapes, out_specs=(anywhere,) * len(shapes),
            compiler_params=params, name="unset",
        )()

    def after(arrays, *others):
        taken = [pltpu.with_memory_space_constraint(x, pltpu.VMEM) for x in (*arrays, *others)]
        return pl.pallas_call(
            lambda *refs: None,
            out_shape=tuple(pltpu.VMEM(x.shape, x.dtype) for x in arrays),
            in_specs=[anywhere] * len(taken),
            out_specs=(anywhere,) * len(arrays),
            input_output_aliases={i: i for i in range(len(arrays))},
            name="after",
        )(*taken)

    xs, zs = lax.axis_size("gx"), lax.axis_size("gz")
    gx = lax.axis_index("gx")
    steps = step_pairs(xs, zs)
    rest = range(1, xs)

    def early_swaps(out, into, held, old):
        part, base = inner(held, old)
        arrays = (held, swap(out, 1, [0]), swap(into, 0, [0]))
        terms = pl.pallas_call(
            edges_kernel,
            out_shape=edge,
            in_specs=[whole] * 3,
            out_specs=whole,
            scratch_shapes=[margins, margins],
            compiler_params=params,
            name="edges",
        )(*(pltpu.with_memory_space_constraint(x, pltpu.VMEM) for x in arrays))
        return terms, part, base

    def early_none(out, into, held, old):
        return unset(edge, block, block)

    def late_swaps(out, into, held, old):
        part, base = inner(held, old)
        return (*after((swap(out, 1, rest), swap(into, 0, rest))), part, base)

    def none(out, into, held, old):
        return unset(halo, halo, block, block)

    second = permute(second, steps[1])
    first = permute(first, steps[0])
    early = lax.cond(gx == 0, early_swaps, early_none, outward, inward, held, old_rhs)
    (third,) = after((third,), early[0])
    third = permute(third, steps[2])
    late = lax.cond(gx == 0, none, late_swaps, outward, inward, held, old_rhs)
    scratch = pltpu.VMEM(velocity.shape, f32)
    sems = pltpu.SemaphoreType.DMA((2 * fields,))

    def last(kernel, arrays, loose, scratches, **more):
        spaces = [pltpu.VMEM] * len(arrays) + [pl.ANY] * len(loose)
        return pl.pallas_call(
            kernel,
            out_shape=(result, result),
            in_specs=[pl.BlockSpec(memory_space=x) for x in spaces],
            out_specs=(anywhere, anywhere),
            scratch_shapes=scratches,
            compiler_params=params,
            **more,
        )(*(pltpu.with_memory_space_constraint(x, pltpu.VMEM) for x in arrays), *loose)

    before = last(
        lowest_kernel, (held, first, second, *early[1:], early[0]), (late[0],), [scratch, scratch, sems], name="lowest",
    )
    new_velocity, right_side = last(
        outer_kernel, (held, first, second, third, *late[2:], *late[:2]), before,
        [scratch, scratch, margins, margins, sems], name="outer", input_output_aliases={8: 0, 9: 1},
    )
    return new_velocity, right_side


def solution(mesh):
    spec = P(None, None, "gz", "gx")
    return jax.shard_map(local, mesh=mesh, in_specs=(spec, spec), out_specs=(spec, spec), check_vma=False)
```

```python
import functools
import math

import jax
import jax.numpy as jnp
from jax import lax
from jax.experimental import pallas as pl
from jax.experimental.pallas import tpu as pltpu
from jax.sharding import PartitionSpec as P

first_alpha = 1.0 / 3.0
first_near = 14.0 / 9.0
first_far = 1.0 / 9.0
second_alpha = 2.0 / 11.0
second_near = 12.0 / 11.0
second_far = 3.0 / 11.0
viscosity = 0.2
time_step = 0.25
gamma_now = 5.0 / 12.0
zeta_old = -17.0 / 60.0
first_stencil = (
    (1, 0.5 * first_near),
    (-1, -0.5 * first_near),
    (2, 0.25 * first_far),
    (-2, -0.25 * first_far),
)
second_stencil = (
    (0, -2.0 * second_near - 0.5 * second_far),
    (1, second_near),
    (-1, second_near),
    (2, 0.25 * second_far),
    (-2, 0.25 * second_far),
)
span_odd = (45.0 / 60.0, -9.0 / 60.0, 1.0 / 60.0)
span_even = (270.0 / 180.0, -27.0 / 180.0, 2.0 / 180.0)
span_centre = -490.0 / 180.0


def green(off_diag):
    root = (-1.0 + math.sqrt(1.0 - 4.0 * off_diag * off_diag)) / (2.0 * off_diag)
    return root, 1.0 / (1.0 + 2.0 * off_diag * root)


def weight_at(distance, stencil, off_diag):
    root, lead = green(off_diag)
    return sum(w * lead * root ** abs(distance + o) for o, w in stencil)


def reach_of(stencil, off_diag):
    root, lead = green(off_diag)
    return lead * sum(w * root**o for o, w in stencil)


def decay(away, off_diag):
    power = jnp.exp(away.astype(jnp.float32) * math.log(-green(off_diag)[0]))
    return jnp.where((away & 1) == 1, -power, power)


def block_matrix(stencil, off_diag, extent, odd):
    row = lax.broadcasted_iota(jnp.int32, (extent, extent), 0)
    column = lax.broadcasted_iota(jnp.int32, (extent, extent), 1)
    away = jnp.abs(column - row)
    far = reach_of(stencil, off_diag) * decay(away, off_diag)
    weight = jnp.where(away == 0, weight_at(0, stencil, off_diag), jnp.where(away == 1, weight_at(1, stencil, off_diag), far))
    if odd:
        weight = jnp.where(column < row, -weight, weight)
    half = jnp.concatenate(split(weight), 1)
    return jnp.concatenate([half, half], 0)


def outer_table(extent):
    row = lax.broadcasted_iota(jnp.int32, (16, 2 * extent), 0)
    column = lax.broadcasted_iota(jnp.int32, (16, 2 * extent), 1)
    left = row < 5
    kind = jnp.where(left, row, row - 5)
    slope = column < extent
    cell = jnp.where(slope, column, column - extent)
    away = jnp.where(left, cell + 1, extent - cell)
    sign = jnp.where(left, 1.0, -1.0)
    reach1, reach2 = reach_of(first_stencil, first_alpha), reach_of(second_stencil, second_alpha)
    near1 = weight_at(1, first_stencil, first_alpha) - reach1 * green(first_alpha)[0]
    near2 = weight_at(1, second_stencil, second_alpha) - reach2 * green(second_alpha)[0]
    touch = (away == 1).astype(jnp.float32)
    far1 = sign * reach1 * decay(away, first_alpha)
    far2 = viscosity * reach2 * decay(away, second_alpha)
    slopes = jnp.where(kind == 0, far1, jnp.where(kind == 2, sign * near1 * touch, 0.0))
    rests = jnp.where(kind == 1, far2, jnp.where(kind == 2, viscosity * near2 * touch, 0.0))
    rests = jnp.where(kind == 3, -0.5 * far1, jnp.where(kind == 4, -0.5 * sign * near1 * touch, rests))
    high, low = split(jnp.where(slope, slopes, rests))
    return jnp.concatenate([high, high, low], 0)


def split(values):
    high = values.astype(jnp.bfloat16)
    low = (values - high.astype(jnp.float32)).astype(jnp.bfloat16)
    return high, low


def moments_kernel(vel_ref, held_ref, first_ref, second_ref, third_ref, outward_ref, inward_ref, sems):
    fields, planes, rows, cols = vel_ref.shape
    lines = planes * rows
    copies = [
        [pltpu.make_async_copy(vel_ref.at[i, p], held_ref.at[i, p], sems.at[planes * i + p]) for p in range(planes)]
        for i in range(fields)
    ]
    for i in range(fields):
        for copy in copies[i]:
            copy.start()
    row = lax.broadcasted_iota(jnp.int32, (8, cols), 0)
    cell = lax.broadcasted_iota(jnp.int32, (8, cols), 1)
    away = jnp.where(row < 3, cell, cols - 1 - cell)
    kind = jnp.where(row < 3, row, row - 3)
    power = jnp.where(kind == 0, decay(away, first_alpha), decay(away, second_alpha))
    table = jnp.where(kind == 2, (away == 0).astype(jnp.float32), jnp.where(kind > 2, 0.0, power))
    high, low = split(table)
    both = jnp.concatenate([high, low], 0)
    gx, gz = lax.axis_index("gx"), lax.axis_index("gz")
    odd = lax.rem(gz, 2)
    xs, zs = lax.axis_size("gx"), lax.axis_size("gz")
    ups = upward_steps(gx, gz, xs, zs)
    inward_first, outward_third = place_of(gx, gz, xs, zs)
    nt = (((1,), (1,)), ((), ()))

    for i in range(fields):
        for copy in copies[i]:
            copy.wait()
    u = held_ref[0].reshape(lines, cols)
    v = held_ref[...].reshape(fields * lines, cols)
    terms = [v] + [u * held_ref[i].reshape(lines, cols) for i in range(fields)]
    near, rest = split(jnp.concatenate(terms, 0))
    all_got = lax.dot_general(both, near, nt, preferred_element_type=jnp.float32)
    rest_got = lax.dot_general(high, rest, nt, preferred_element_type=jnp.float32)
    all_got = all_got[:8] + all_got[8:] + rest_got
    for i in range(fields):
        got = all_got[:, i * lines : (i + 1) * lines]
        flux = all_got[:, (fields + i) * lines : (fields + i + 1) * lines]
        at = slice(i * lines, (i + 1) * lines)
        lower = jnp.concatenate([got[0:3], flux[0:1]], 0)
        upper = jnp.concatenate([got[3:6], flux[3:4]], 0)
        for row in range(4):
            for half in range(2):
                near = slice(half * cols, (half + 1) * cols)
                below, above = lower[row : row + 1, near], upper[row : row + 1, near]
                first_ref[i, row, half : half + 1] = jnp.where(ups[0], above, below)
                second_ref[i, row, half : half + 1] = jnp.where(ups[1], above, below)
                third_ref[i, row, half : half + 1] = below
        head, tail = held_ref[i, :, :3], held_ref[i, :, rows - 3 :]
        inward_ref[i] = jnp.where(odd == 0, tail, head)
        outward_ref[i] = jnp.where(odd == 0, head, tail)

    @pl.when(outward_third)
    def _():
        third_ref[...] = outward_ref[...]

    @pl.when(inward_first)
    def _():
        first_ref[...] = inward_ref[...]


def mul_split(values, table):
    high, low = split(values)
    got = jnp.dot(jnp.concatenate([high, low], 1), table, preferred_element_type=jnp.float32)
    half = table.shape[1] // 2
    return got[:, :half] + got[:, half:]


def shifted(values, offset):
    planes, rows, cols = values.shape
    zeros = jnp.zeros((planes, abs(offset), cols), values.dtype)
    if offset > 0:
        return jnp.concatenate([values[:, offset:], zeros], 1)
    return jnp.concatenate([zeros, values[:, :offset]], 1)


def span_tap(v_far, w_near, w_far, distance, sign):
    odd = -0.5 * sign * span_odd[distance - 1]
    even = viscosity * span_even[distance - 1]
    return v_far * (odd * (w_near + w_far) + even)


def inner_kernel(vel_ref, old_ref, part_ref, base_ref, kept_ref, sem):
    copy = pltpu.make_async_copy(old_ref, kept_ref, sem)
    copy.start()
    planes, rows, cols = vel_ref.shape[1:]
    lines = planes * rows
    u = vel_ref[0].reshape(lines, cols)
    w = vel_ref[2]
    first = block_matrix(first_stencil, first_alpha, cols, True)
    second = block_matrix(second_stencil, second_alpha, cols, False)
    for i in range(3):
        v3 = vel_ref[i]
        v = v3.reshape(lines, cols)
        slope = mul_split(v, first)
        curve = mul_split(v, second)
        flux = mul_split(u * v, first)
        total = -0.5 * (u * slope + flux) + viscosity * curve
        total = total.reshape(planes, rows, cols) + (viscosity * span_centre) * v3
        for distance in (1, 2, 3):
            for sign in (1, -1):
                offset = sign * distance
                total = total + span_tap(shifted(v3, offset), w, shifted(w, offset), distance, sign)
        part_ref[i] = total
    copy.wait()
    for i in range(3):
        fresh = (time_step * gamma_now) * part_ref[i] + (time_step * zeta_old) * kept_ref[i]
        base_ref[i] = vel_ref[i] + fresh


def set_margins(outward, inward, below_ref, above_ref):
    odd = lax.rem(lax.axis_index("gz"), 2) == 1
    below_ref[...] = jnp.zeros(below_ref.shape, jnp.float32)
    above_ref[...] = jnp.zeros(above_ref.shape, jnp.float32)
    below_ref[:, :, 0:3] = jnp.where(odd, inward, outward)
    above_ref[:, :, 8:11] = jnp.where(odd, outward, inward)


def edge_terms(vel_ref, below_ref, above_ref, i):
    rows = vel_ref.shape[2]
    w_low, w_high = vel_ref[2, :, 0:8], vel_ref[2, :, rows - 8 :]
    low, high = 0.0, 0.0
    for d in (1, 2, 3):
        near = slice(3 - d, 11 - d)
        low = low + span_tap(below_ref[i, :, near], w_low, below_ref[2, :, near], d, -1)
        near = slice(d, d + 8)
        high = high + span_tap(above_ref[i, :, near], w_high, above_ref[2, :, near], d, 1)
    return low, high


def edges_kernel(vel_ref, outward_ref, inward_ref, edges_ref, below_ref, above_ref):
    set_margins(outward_ref[...], inward_ref[...], below_ref, above_ref)
    for i in range(vel_ref.shape[0]):
        edges_ref[i, :, 0:8], edges_ref[i, :, 8:16] = edge_terms(vel_ref, below_ref, above_ref, i)


def lowest_kernel(
    vel_ref, first_ref, second_ref, part_ref, base_ref, edges_ref, late_ref,
    new_ref, rhs_ref, new_held, rhs_held, sems
):
    @pl.when(lax.axis_index("gx") == 0)
    def _():
        finish(
            vel_ref, first_ref, second_ref, None, part_ref, base_ref,
            lambda i: (edges_ref[i, :, 0:8], edges_ref[i, :, 8:16]),
            new_ref, rhs_ref, new_held, rhs_held, sems
        )


def outer_kernel(
    vel_ref, first_ref, second_ref, third_ref, part_ref, base_ref, outward_ref, inward_ref, new_before, rhs_before,
    new_ref, rhs_ref, new_held, rhs_held, below_ref, above_ref, sems
):
    @pl.when(lax.axis_index("gx") > 0)
    def _():
        gx, gz = lax.axis_index("gx"), lax.axis_index("gz")
        inward_first, outward_third = place_of(gx, gz, lax.axis_size("gx"), lax.axis_size("gz"))
        outward = jnp.where(outward_third, third_ref[...], outward_ref[...])
        inward = jnp.where(inward_first, first_ref[...], inward_ref[...])
        set_margins(outward, inward, below_ref, above_ref)
        finish(
            vel_ref, first_ref, second_ref, third_ref, part_ref, base_ref,
            functools.partial(edge_terms, vel_ref, below_ref, above_ref),
            new_ref, rhs_ref, new_held, rhs_held, sems
        )


def finish(
    vel_ref, first_ref, second_ref, third_ref, part_ref, base_ref, edges,
    new_ref, rhs_ref, new_held, rhs_held, sems
):
    fields, planes, rows, cols = vel_ref.shape
    lines = planes * rows
    u = vel_ref[0].reshape(lines, cols)
    gx, gz = lax.axis_index("gx"), lax.axis_index("gz")
    xs, zs = lax.axis_size("gx"), lax.axis_size("gz")
    third = None if third_ref is None else gathered(third_ref)
    left, right = arrivals(gx, gz, xs, zs, gathered(first_ref), gathered(second_ref), third)
    u_edge = (left[2:3, :lines], right[2:3, :lines])
    table = outer_table(cols)
    tn = (((0,), (0,)), ((), ()))
    copies = []

    def across(i):
        at = slice(i * lines, (i + 1) * lines)
        pieces = []
        for side, got in ((0, left[:, at]), (1, right[:, at])):
            pieces += [got, got[2:3] * u_edge[side]]
        pieces.append(jnp.zeros((6, lines), jnp.float32))
        high, low = split(jnp.concatenate(pieces, 0))
        spread = lax.dot_general(
            jnp.concatenate([high, low, high], 0), table, tn, preferred_element_type=jnp.float32
        )
        extra = (spread[:, cols:] - 0.5 * u * spread[:, :cols]).reshape(planes, rows, cols)
        rhs_held[i] = part_ref[i] + extra
        new_held[i] = base_ref[i] + (time_step * gamma_now) * extra

    def along(i):
        low_fix, high_fix = edges(i)
        for at, fix in ((slice(0, 8), low_fix), (slice(rows - 8, rows), high_fix)):
            rhs_held[i, :, at] += fix
            new_held[i, :, at] += (time_step * gamma_now) * fix
        for k, (source, target) in enumerate(((rhs_held, rhs_ref), (new_held, new_ref))):
            copies.append(pltpu.make_async_copy(source.at[i], target.at[i], sems.at[2 * i + k]))
            copies[-1].start()

    for i in range(fields):
        across(i)
        along(i)
    for copy in copies:
        copy.wait()


def place_of(gx, gz, xs, zs):
    inward = jnp.logical_and(gz <= 1, jnp.logical_and(gx >= 3, gx <= xs - 2))
    outward = jnp.logical_and(jnp.logical_or(gz == 0, gz == zs - 1), gx == 1)
    return inward, outward


def upward_steps(gx, gz, xs, zs):
    low, top = gz == 0, gz == zs - 1
    first = jnp.where(low, jnp.logical_or(gx == 1, gx == xs - 1), jnp.logical_or(top, gx == 0))
    down = jnp.logical_or(jnp.logical_and(low, gx == 1), jnp.logical_and(top, jnp.logical_or(gx == 1, gx == 2)))
    return first, jnp.logical_not(down)


def step_pairs(xs, zs):
    up = lambda x, z: ((x, z), ((x + 1) % xs, z))
    down = lambda x, z: ((x, z), ((x - 1) % xs, z))
    top = zs - 1
    first = [up(1, 0), down(2, 0), up(xs - 1, 0)] + [up(x, top) for x in (0, 1, 2, xs - 1)]
    second = [up(0, 0), down(1, 0), down(1, top), down(2, top)]
    second += [up(x, 0) for x in range(2, xs - 1)] + [up(x, top) for x in range(3, xs - 1)]
    third = [down(x, z) for z in (0, top) for x in (0, *range(3, xs))]
    for z in range(1, top):
        first += [up(0, z), down(1, z)]
        second += [up(x, z) for x in range(1, xs)]
        third += [down(x, z) for x in range(2, xs)] + [down(0, z)]
    for x in range(3, xs - 1):
        first += [((x, 0), (x, 1)), ((x, 1), (x, 0))]
    third += [((1, 0), (1, top)), ((1, top), (1, 0))]
    return first, second, third


def arrivals(gx, gz, xs, zs, first, second, third):
    low, top = gz == 0, gz == zs - 1
    if third is None:
        side = jnp.logical_or(low, top)
        return jnp.where(side, first, second), jnp.where(side, second, first)
    left = jnp.where(jnp.where(low, gx == 2, jnp.where(top, gx <= 3, gx == 1)), first, second)
    right = jnp.where(jnp.logical_and(low, gx == 1), first, third)
    return left, jnp.where(jnp.logical_and(top, gx == 1), second, right)


def gathered(ref):
    fields = ref.shape[0]
    return jnp.concatenate(
        [
            jnp.concatenate([ref[i, row, half : half + 1] for i in range(fields) for half in range(2)], 1)
            for row in range(4)
        ],
        0,
    )


def permute(values, pairs):
    count = lax.axis_size("gz")
    return lax.ppermute(values, ("gx", "gz"), [(a * count + b, c * count + d) for (a, b), (c, d) in pairs])


def swap(values, first, blocks, done=()):
    count = lax.axis_size("gz")
    pairs = []
    for x in blocks:
        for i in range(count // 2):
            a, b = ((x, (2 * i + k + first) % count) for k in (0, 1))
            if x not in done or (a[1] > 0 and b[1] > 0):
                pairs += [(a, b), (b, a)]
    return permute(values, pairs)


def local(velocity, old_rhs):
    fields, planes, rows, cols = velocity.shape
    lines = planes * rows
    anywhere = pl.BlockSpec(memory_space=pl.ANY)
    whole = pl.BlockSpec(memory_space=pltpu.VMEM)
    f32 = jnp.float32
    block = pltpu.VMEM(velocity.shape, f32)
    side = pltpu.VMEM((4, fields * lines), f32)
    halo = pltpu.VMEM((fields, planes, 3, cols), f32)
    edge = pltpu.VMEM((fields, planes, 16, cols), f32)
    margins = edge
    result = jax.ShapeDtypeStruct(velocity.shape, f32)
    params = pltpu.CompilerParams(vmem_limit_bytes=32 * 1024 * 1024)

    held, first, second, third, outward, inward = pl.pallas_call(
        moments_kernel,
        out_shape=(block, halo, halo, halo, halo, halo),
        in_specs=[pl.BlockSpec(memory_space=pltpu.HBM)],
        out_specs=(whole,) * 6,
        scratch_shapes=[pltpu.SemaphoreType.DMA((fields * planes,))],
        compiler_params=params,
        name="moments",
    )(pltpu.with_memory_space_constraint(velocity, pltpu.HBM))

    def inner(held, old):
        return pl.pallas_call(
            inner_kernel,
            out_shape=(block, block),
            in_specs=[whole, pl.BlockSpec(memory_space=pltpu.HBM)],
            out_specs=(whole, whole),
            scratch_shapes=[pltpu.VMEM(velocity.shape, f32), pltpu.SemaphoreType.DMA],
            compiler_params=params,
            cost_estimate=pl.CostEstimate(flops=600_000_000, bytes_accessed=1_000_000, transcendentals=0),
            name="inner",
        )(pltpu.with_memory_space_constraint(held, pltpu.VMEM), pltpu.with_memory_space_constraint(old, pltpu.HBM))

    def unset(*shapes):
        return pl.pallas_call(
            lambda *refs: None, out_shape=shapes, out_specs=(anywhere,) * len(shapes),
            compiler_params=params, name="unset",
        )()

    def after(arrays, *others):
        taken = [pltpu.with_memory_space_constraint(x, pltpu.VMEM) for x in (*arrays, *others)]
        return pl.pallas_call(
            lambda *refs: None,
            out_shape=tuple(pltpu.VMEM(x.shape, x.dtype) for x in arrays),
            in_specs=[anywhere] * len(taken),
            out_specs=(anywhere,) * len(arrays),
            input_output_aliases={i: i for i in range(len(arrays))},
            name="after",
        )(*taken)

    xs, zs = lax.axis_size("gx"), lax.axis_size("gz")
    gx = lax.axis_index("gx")
    steps = step_pairs(xs, zs)
    rest = range(1, xs)

    def early_swaps(out, into, held, old):
        part, base = inner(held, old)
        arrays = (held, swap(out, 1, [0]), swap(into, 0, [0]))
        terms = pl.pallas_call(
            edges_kernel,
            out_shape=edge,
            in_specs=[whole] * 3,
            out_specs=whole,
            scratch_shapes=[margins, margins],
            compiler_params=params,
            name="edges",
        )(*(pltpu.with_memory_space_constraint(x, pltpu.VMEM) for x in arrays))
        return terms, part, base

    def early_none(out, into, held, old):
        return unset(edge, block, block)

    def late_swaps(out, into, held, old):
        part, base = inner(held, old)
        return (*after((swap(out, 1, rest, (1,)), swap(into, 0, rest, range(3, xs - 1)))), part, base)

    def none(out, into, held, old):
        return unset(halo, halo, block, block)

    second = permute(second, steps[1])
    first = permute(first, steps[0])
    early = lax.cond(gx == 0, early_swaps, early_none, outward, inward, held, old_rhs)
    (third,) = after((third,), early[0])
    third = permute(third, steps[2])
    late = lax.cond(gx == 0, none, late_swaps, outward, inward, held, old_rhs)
    scratch = pltpu.VMEM(velocity.shape, f32)
    sems = pltpu.SemaphoreType.DMA((2 * fields,))

    def last(kernel, arrays, loose, scratches, **more):
        spaces = [pltpu.VMEM] * len(arrays) + [pl.ANY] * len(loose)
        return pl.pallas_call(
            kernel,
            out_shape=(result, result),
            in_specs=[pl.BlockSpec(memory_space=x) for x in spaces],
            out_specs=(anywhere, anywhere),
            scratch_shapes=scratches,
            compiler_params=params,
            **more,
        )(*(pltpu.with_memory_space_constraint(x, pltpu.VMEM) for x in arrays), *loose)

    before = last(
        lowest_kernel, (held, first, second, *early[1:], early[0]), (late[0],), [scratch, scratch, sems], name="lowest",
    )
    new_velocity, right_side = last(
        outer_kernel, (held, first, second, third, *late[2:], *late[:2]), before,
        [scratch, scratch, margins, margins, sems], name="outer", input_output_aliases={8: 0, 9: 1},
    )
    return new_velocity, right_side


def solution(mesh):
    spec = P(None, None, "gz", "gx")
    return jax.shard_map(local, mesh=mesh, in_specs=(spec, spec), out_specs=(spec, spec), check_vma=False)
```

```python
import functools
import math

import jax
import jax.numpy as jnp
from jax import lax
from jax.experimental import pallas as pl
from jax.experimental.pallas import tpu as pltpu
from jax.sharding import PartitionSpec as P

first_alpha = 1.0 / 3.0
first_near = 14.0 / 9.0
first_far = 1.0 / 9.0
second_alpha = 2.0 / 11.0
second_near = 12.0 / 11.0
second_far = 3.0 / 11.0
viscosity = 0.2
time_step = 0.25
gamma_now = 5.0 / 12.0
zeta_old = -17.0 / 60.0
first_stencil = (
    (1, 0.5 * first_near),
    (-1, -0.5 * first_near),
    (2, 0.25 * first_far),
    (-2, -0.25 * first_far),
)
second_stencil = (
    (0, -2.0 * second_near - 0.5 * second_far),
    (1, second_near),
    (-1, second_near),
    (2, 0.25 * second_far),
    (-2, 0.25 * second_far),
)
span_odd = (45.0 / 60.0, -9.0 / 60.0, 1.0 / 60.0)
span_even = (270.0 / 180.0, -27.0 / 180.0, 2.0 / 180.0)
span_centre = -490.0 / 180.0


def green(off_diag):
    root = (-1.0 + math.sqrt(1.0 - 4.0 * off_diag * off_diag)) / (2.0 * off_diag)
    return root, 1.0 / (1.0 + 2.0 * off_diag * root)


def weight_at(distance, stencil, off_diag):
    root, lead = green(off_diag)
    return sum(w * lead * root ** abs(distance + o) for o, w in stencil)


def reach_of(stencil, off_diag):
    root, lead = green(off_diag)
    return lead * sum(w * root**o for o, w in stencil)


def decay(away, off_diag):
    power = jnp.exp(away.astype(jnp.float32) * math.log(-green(off_diag)[0]))
    return jnp.where((away & 1) == 1, -power, power)


def block_matrix(stencil, off_diag, extent, odd):
    row = lax.broadcasted_iota(jnp.int32, (extent, extent), 0)
    column = lax.broadcasted_iota(jnp.int32, (extent, extent), 1)
    away = jnp.abs(column - row)
    far = reach_of(stencil, off_diag) * decay(away, off_diag)
    weight = jnp.where(away == 0, weight_at(0, stencil, off_diag), jnp.where(away == 1, weight_at(1, stencil, off_diag), far))
    if odd:
        weight = jnp.where(column < row, -weight, weight)
    half = jnp.concatenate(split(weight), 1)
    return jnp.concatenate([half, half], 0)


def outer_table(extent):
    row = lax.broadcasted_iota(jnp.int32, (16, 2 * extent), 0)
    column = lax.broadcasted_iota(jnp.int32, (16, 2 * extent), 1)
    left = row < 5
    kind = jnp.where(left, row, row - 5)
    slope = column < extent
    cell = jnp.where(slope, column, column - extent)
    away = jnp.where(left, cell + 1, extent - cell)
    sign = jnp.where(left, 1.0, -1.0)
    reach1, reach2 = reach_of(first_stencil, first_alpha), reach_of(second_stencil, second_alpha)
    near1 = weight_at(1, first_stencil, first_alpha) - reach1 * green(first_alpha)[0]
    near2 = weight_at(1, second_stencil, second_alpha) - reach2 * green(second_alpha)[0]
    touch = (away == 1).astype(jnp.float32)
    far1 = sign * reach1 * decay(away, first_alpha)
    far2 = viscosity * reach2 * decay(away, second_alpha)
    slopes = jnp.where(kind == 0, far1, jnp.where(kind == 2, sign * near1 * touch, 0.0))
    rests = jnp.where(kind == 1, far2, jnp.where(kind == 2, viscosity * near2 * touch, 0.0))
    rests = jnp.where(kind == 3, -0.5 * far1, jnp.where(kind == 4, -0.5 * sign * near1 * touch, rests))
    return jnp.where(slope, slopes, rests)


def split(values):
    high = values.astype(jnp.bfloat16)
    low = (values - high.astype(jnp.float32)).astype(jnp.bfloat16)
    return high, low


def moments_kernel(vel_ref, held_ref, first_ref, second_ref, third_ref, outward_ref, inward_ref, profiles_ref, sems):
    fields, planes, rows, cols = vel_ref.shape
    lines = planes * rows
    copies = [
        [pltpu.make_async_copy(vel_ref.at[i, p], held_ref.at[i, p], sems.at[planes * i + p]) for p in range(planes)]
        for i in range(fields)
    ]
    for i in range(fields):
        for copy in copies[i]:
            copy.start()
    profiles_ref[...] = outer_table(cols)
    row = lax.broadcasted_iota(jnp.int32, (8, cols), 0)
    cell = lax.broadcasted_iota(jnp.int32, (8, cols), 1)
    away = jnp.where(row < 3, cell, cols - 1 - cell)
    kind = jnp.where(row < 3, row, row - 3)
    power = jnp.where(kind == 0, decay(away, first_alpha), decay(away, second_alpha))
    table = jnp.where(kind == 2, (away == 0).astype(jnp.float32), jnp.where(kind > 2, 0.0, power))
    high, low = split(table)
    both = jnp.concatenate([high, low], 0)
    gx, gz = lax.axis_index("gx"), lax.axis_index("gz")
    odd = lax.rem(gz, 2)
    xs, zs = lax.axis_size("gx"), lax.axis_size("gz")
    ups = upward_steps(gx, gz, xs, zs)
    inward_first, outward_third = place_of(gx, gz, xs, zs)
    nt = (((1,), (1,)), ((), ()))

    for i in range(fields):
        for copy in copies[i]:
            copy.wait()
    u = held_ref[0].reshape(lines, cols)
    v = held_ref[...].reshape(fields * lines, cols)
    terms = [v] + [u * held_ref[i].reshape(lines, cols) for i in range(fields)]
    near, rest = split(jnp.concatenate(terms, 0))
    all_got = lax.dot_general(both, near, nt, preferred_element_type=jnp.float32)
    rest_got = lax.dot_general(high, rest, nt, preferred_element_type=jnp.float32)
    all_got = all_got[:8] + all_got[8:] + rest_got
    for i in range(fields):
        got = all_got[:, i * lines : (i + 1) * lines]
        flux = all_got[:, (fields + i) * lines : (fields + i + 1) * lines]
        at = slice(i * lines, (i + 1) * lines)
        lower = jnp.concatenate([got[0:3], flux[0:1]], 0)
        upper = jnp.concatenate([got[3:6], flux[3:4]], 0)
        for row in range(4):
            for half in range(2):
                near = slice(half * cols, (half + 1) * cols)
                below, above = lower[row : row + 1, near], upper[row : row + 1, near]
                first_ref[i, row, half : half + 1] = jnp.where(ups[0], above, below)
                second_ref[i, row, half : half + 1] = jnp.where(ups[1], above, below)
                third_ref[i, row, half : half + 1] = below
        head, tail = held_ref[i, :, :3], held_ref[i, :, rows - 3 :]
        inward_ref[i] = jnp.where(odd == 0, tail, head)
        outward_ref[i] = jnp.where(odd == 0, head, tail)

    @pl.when(outward_third)
    def _():
        third_ref[...] = outward_ref[...]

    @pl.when(inward_first)
    def _():
        first_ref[...] = inward_ref[...]


def mul_split(values, table):
    high, low = split(values)
    got = jnp.dot(jnp.concatenate([high, low], 1), table, preferred_element_type=jnp.float32)
    half = table.shape[1] // 2
    return got[:, :half] + got[:, half:]


def shifted(values, offset):
    planes, rows, cols = values.shape
    zeros = jnp.zeros((planes, abs(offset), cols), values.dtype)
    if offset > 0:
        return jnp.concatenate([values[:, offset:], zeros], 1)
    return jnp.concatenate([zeros, values[:, :offset]], 1)


def span_tap(v_far, w_near, w_far, distance, sign):
    odd = -0.5 * sign * span_odd[distance - 1]
    even = viscosity * span_even[distance - 1]
    return v_far * (odd * (w_near + w_far) + even)


def inner_kernel(vel_ref, old_ref, part_ref, base_ref, kept_ref, sem):
    copy = pltpu.make_async_copy(old_ref, kept_ref, sem)
    copy.start()
    planes, rows, cols = vel_ref.shape[1:]
    lines = planes * rows
    u = vel_ref[0].reshape(lines, cols)
    w = vel_ref[2]
    first = block_matrix(first_stencil, first_alpha, cols, True)
    second = block_matrix(second_stencil, second_alpha, cols, False)
    for i in range(3):
        v3 = vel_ref[i]
        v = v3.reshape(lines, cols)
        slope = mul_split(v, first)
        curve = mul_split(v, second)
        flux = mul_split(u * v, first)
        total = -0.5 * (u * slope + flux) + viscosity * curve
        total = total.reshape(planes, rows, cols) + (viscosity * span_centre) * v3
        for distance in (1, 2, 3):
            for sign in (1, -1):
                offset = sign * distance
                total = total + span_tap(shifted(v3, offset), w, shifted(w, offset), distance, sign)
        part_ref[i] = total
    copy.wait()
    for i in range(3):
        fresh = (time_step * gamma_now) * part_ref[i] + (time_step * zeta_old) * kept_ref[i]
        base_ref[i] = vel_ref[i] + fresh


def set_margins(outward, inward, below_ref, above_ref):
    odd = lax.rem(lax.axis_index("gz"), 2) == 1
    below_ref[...] = jnp.zeros(below_ref.shape, jnp.float32)
    above_ref[...] = jnp.zeros(above_ref.shape, jnp.float32)
    below_ref[:, :, 0:3] = jnp.where(odd, inward, outward)
    above_ref[:, :, 8:11] = jnp.where(odd, outward, inward)


def edge_terms(vel_ref, below_ref, above_ref, i):
    rows = vel_ref.shape[2]
    w_low, w_high = vel_ref[2, :, 0:8], vel_ref[2, :, rows - 8 :]
    low, high = 0.0, 0.0
    for d in (1, 2, 3):
        near = slice(3 - d, 11 - d)
        low = low + span_tap(below_ref[i, :, near], w_low, below_ref[2, :, near], d, -1)
        near = slice(d, d + 8)
        high = high + span_tap(above_ref[i, :, near], w_high, above_ref[2, :, near], d, 1)
    return low, high


def edges_kernel(vel_ref, outward_ref, inward_ref, edges_ref, below_ref, above_ref):
    set_margins(outward_ref[...], inward_ref[...], below_ref, above_ref)
    for i in range(vel_ref.shape[0]):
        edges_ref[i, :, 0:8], edges_ref[i, :, 8:16] = edge_terms(vel_ref, below_ref, above_ref, i)


def lowest_kernel(
    vel_ref, first_ref, second_ref, part_ref, base_ref, edges_ref, profiles_ref, late_ref,
    new_ref, rhs_ref, new_held, rhs_held, sems
):
    @pl.when(lax.axis_index("gx") == 0)
    def _():
        finish(
            vel_ref, first_ref, second_ref, None, part_ref, base_ref,
            lambda i: (edges_ref[i, :, 0:8], edges_ref[i, :, 8:16]), profiles_ref,
            new_ref, rhs_ref, new_held, rhs_held, sems
        )


def outer_kernel(
    vel_ref, first_ref, second_ref, third_ref, part_ref, base_ref, outward_ref, inward_ref, profiles_ref, new_before, rhs_before,
    new_ref, rhs_ref, new_held, rhs_held, below_ref, above_ref, sems
):
    @pl.when(lax.axis_index("gx") > 0)
    def _():
        gx, gz = lax.axis_index("gx"), lax.axis_index("gz")
        inward_first, outward_third = place_of(gx, gz, lax.axis_size("gx"), lax.axis_size("gz"))
        outward = jnp.where(outward_third, third_ref[...], outward_ref[...])
        inward = jnp.where(inward_first, first_ref[...], inward_ref[...])
        set_margins(outward, inward, below_ref, above_ref)
        finish(
            vel_ref, first_ref, second_ref, third_ref, part_ref, base_ref,
            functools.partial(edge_terms, vel_ref, below_ref, above_ref), profiles_ref,
            new_ref, rhs_ref, new_held, rhs_held, sems
        )


def finish(
    vel_ref, first_ref, second_ref, third_ref, part_ref, base_ref, edges, profiles_ref,
    new_ref, rhs_ref, new_held, rhs_held, sems
):
    fields, planes, rows, cols = vel_ref.shape
    lines = planes * rows
    u = vel_ref[0].reshape(lines, cols)
    gx, gz = lax.axis_index("gx"), lax.axis_index("gz")
    xs, zs = lax.axis_size("gx"), lax.axis_size("gz")
    third = None if third_ref is None else gathered(third_ref)
    left, right = arrivals(gx, gz, xs, zs, gathered(first_ref), gathered(second_ref), third)
    u_edge = (left[2:3, :lines], right[2:3, :lines])
    high, low = split(profiles_ref[...])
    table = jnp.concatenate([high, high, low], 0)
    tn = (((0,), (0,)), ((), ()))
    copies = []

    def across(i):
        at = slice(i * lines, (i + 1) * lines)
        pieces = []
        for side, got in ((0, left[:, at]), (1, right[:, at])):
            pieces += [got, got[2:3] * u_edge[side]]
        pieces.append(jnp.zeros((6, lines), jnp.float32))
        high, low = split(jnp.concatenate(pieces, 0))
        spread = lax.dot_general(
            jnp.concatenate([high, low, high], 0), table, tn, preferred_element_type=jnp.float32
        )
        extra = (spread[:, cols:] - 0.5 * u * spread[:, :cols]).reshape(planes, rows, cols)
        rhs_held[i] = part_ref[i] + extra
        new_held[i] = base_ref[i] + (time_step * gamma_now) * extra

    def along(i):
        low_fix, high_fix = edges(i)
        for at, fix in ((slice(0, 8), low_fix), (slice(rows - 8, rows), high_fix)):
            rhs_held[i, :, at] += fix
            new_held[i, :, at] += (time_step * gamma_now) * fix
        for k, (source, target) in enumerate(((rhs_held, rhs_ref), (new_held, new_ref))):
            copies.append(pltpu.make_async_copy(source.at[i], target.at[i], sems.at[2 * i + k]))
            copies[-1].start()

    for i in range(fields):
        across(i)
        along(i)
    for copy in copies:
        copy.wait()


def place_of(gx, gz, xs, zs):
    inward = jnp.logical_and(gz <= 1, jnp.logical_and(gx >= 3, gx <= xs - 2))
    outward = jnp.logical_and(jnp.logical_or(gz == 0, gz == zs - 1), gx == 1)
    return inward, outward


def upward_steps(gx, gz, xs, zs):
    low, top = gz == 0, gz == zs - 1
    first = jnp.where(low, jnp.logical_or(gx == 1, gx == xs - 1), jnp.logical_or(top, gx == 0))
    down = jnp.logical_or(jnp.logical_and(low, gx == 1), jnp.logical_and(top, jnp.logical_or(gx == 1, gx == 2)))
    return first, jnp.logical_not(down)


def step_pairs(xs, zs):
    up = lambda x, z: ((x, z), ((x + 1) % xs, z))
    down = lambda x, z: ((x, z), ((x - 1) % xs, z))
    top = zs - 1
    first = [up(1, 0), down(2, 0), up(xs - 1, 0)] + [up(x, top) for x in (0, 1, 2, xs - 1)]
    second = [up(0, 0), down(1, 0), down(1, top), down(2, top)]
    second += [up(x, 0) for x in range(2, xs - 1)] + [up(x, top) for x in range(3, xs - 1)]
    third = [down(x, z) for z in (0, top) for x in (0, *range(3, xs))]
    for z in range(1, top):
        first += [up(0, z), down(1, z)]
        second += [up(x, z) for x in range(1, xs)]
        third += [down(x, z) for x in range(2, xs)] + [down(0, z)]
    for x in range(3, xs - 1):
        first += [((x, 0), (x, 1)), ((x, 1), (x, 0))]
    third += [((1, 0), (1, top)), ((1, top), (1, 0))]
    return first, second, third


def arrivals(gx, gz, xs, zs, first, second, third):
    low, top = gz == 0, gz == zs - 1
    if third is None:
        side = jnp.logical_or(low, top)
        return jnp.where(side, first, second), jnp.where(side, second, first)
    left = jnp.where(jnp.where(low, gx == 2, jnp.where(top, gx <= 3, gx == 1)), first, second)
    right = jnp.where(jnp.logical_and(low, gx == 1), first, third)
    return left, jnp.where(jnp.logical_and(top, gx == 1), second, right)


def gathered(ref):
    fields = ref.shape[0]
    return jnp.concatenate(
        [
            jnp.concatenate([ref[i, row, half : half + 1] for i in range(fields) for half in range(2)], 1)
            for row in range(4)
        ],
        0,
    )


def permute(values, pairs):
    count = lax.axis_size("gz")
    return lax.ppermute(values, ("gx", "gz"), [(a * count + b, c * count + d) for (a, b), (c, d) in pairs])


def swap(values, first, blocks, done=()):
    count = lax.axis_size("gz")
    pairs = []
    for x in blocks:
        for i in range(count // 2):
            a, b = ((x, (2 * i + k + first) % count) for k in (0, 1))
            if x not in done or (a[1] > 0 and b[1] > 0):
                pairs += [(a, b), (b, a)]
    return permute(values, pairs)


def local(velocity, old_rhs):
    fields, planes, rows, cols = velocity.shape
    lines = planes * rows
    anywhere = pl.BlockSpec(memory_space=pl.ANY)
    whole = pl.BlockSpec(memory_space=pltpu.VMEM)
    f32 = jnp.float32
    block = pltpu.VMEM(velocity.shape, f32)
    side = pltpu.VMEM((4, fields * lines), f32)
    halo = pltpu.VMEM((fields, planes, 3, cols), f32)
    edge = pltpu.VMEM((fields, planes, 16, cols), f32)
    margins = edge
    result = jax.ShapeDtypeStruct(velocity.shape, f32)
    params = pltpu.CompilerParams(vmem_limit_bytes=32 * 1024 * 1024)

    held, first, second, third, outward, inward, profiles = pl.pallas_call(
        moments_kernel,
        out_shape=(block, halo, halo, halo, halo, halo, pltpu.VMEM((16, 2 * cols), f32)),
        in_specs=[pl.BlockSpec(memory_space=pltpu.HBM)],
        out_specs=(whole,) * 7,
        scratch_shapes=[pltpu.SemaphoreType.DMA((fields * planes,))],
        compiler_params=params,
        name="moments",
    )(pltpu.with_memory_space_constraint(velocity, pltpu.HBM))

    def inner(held, old):
        return pl.pallas_call(
            inner_kernel,
            out_shape=(block, block),
            in_specs=[whole, pl.BlockSpec(memory_space=pltpu.HBM)],
            out_specs=(whole, whole),
            scratch_shapes=[pltpu.VMEM(velocity.shape, f32), pltpu.SemaphoreType.DMA],
            compiler_params=params,
            cost_estimate=pl.CostEstimate(flops=600_000_000, bytes_accessed=1_000_000, transcendentals=0),
            name="inner",
        )(pltpu.with_memory_space_constraint(held, pltpu.VMEM), pltpu.with_memory_space_constraint(old, pltpu.HBM))

    def unset(*shapes):
        return pl.pallas_call(
            lambda *refs: None, out_shape=shapes, out_specs=(anywhere,) * len(shapes),
            compiler_params=params, name="unset",
        )()

    def after(arrays, *others):
        taken = [pltpu.with_memory_space_constraint(x, pltpu.VMEM) for x in (*arrays, *others)]
        return pl.pallas_call(
            lambda *refs: None,
            out_shape=tuple(pltpu.VMEM(x.shape, x.dtype) for x in arrays),
            in_specs=[anywhere] * len(taken),
            out_specs=(anywhere,) * len(arrays),
            input_output_aliases={i: i for i in range(len(arrays))},
            name="after",
        )(*taken)

    xs, zs = lax.axis_size("gx"), lax.axis_size("gz")
    gx = lax.axis_index("gx")
    steps = step_pairs(xs, zs)
    rest = range(1, xs)

    def early_swaps(out, into, held, old):
        part, base = inner(held, old)
        arrays = (held, swap(out, 1, [0]), swap(into, 0, [0]))
        terms = pl.pallas_call(
            edges_kernel,
            out_shape=edge,
            in_specs=[whole] * 3,
            out_specs=whole,
            scratch_shapes=[margins, margins],
            compiler_params=params,
            name="edges",
        )(*(pltpu.with_memory_space_constraint(x, pltpu.VMEM) for x in arrays))
        return terms, part, base

    def early_none(out, into, held, old):
        return unset(edge, block, block)

    def late_swaps(out, into, held, old):
        part, base = inner(held, old)
        return (*after((swap(out, 1, rest, (1,)), swap(into, 0, rest, range(3, xs - 1)))), part, base)

    def none(out, into, held, old):
        return unset(halo, halo, block, block)

    second = permute(second, steps[1])
    first = permute(first, steps[0])
    early = lax.cond(gx == 0, early_swaps, early_none, outward, inward, held, old_rhs)
    (third,) = after((third,), early[0])
    third = permute(third, steps[2])
    late = lax.cond(gx == 0, none, late_swaps, outward, inward, held, old_rhs)
    scratch = pltpu.VMEM(velocity.shape, f32)
    sems = pltpu.SemaphoreType.DMA((2 * fields,))

    def last(kernel, arrays, loose, scratches, **more):
        spaces = [pltpu.VMEM] * len(arrays) + [pl.ANY] * len(loose)
        return pl.pallas_call(
            kernel,
            out_shape=(result, result),
            in_specs=[pl.BlockSpec(memory_space=x) for x in spaces],
            out_specs=(anywhere, anywhere),
            scratch_shapes=scratches,
            compiler_params=params,
            **more,
        )(*(pltpu.with_memory_space_constraint(x, pltpu.VMEM) for x in arrays), *loose)

    before = last(
        lowest_kernel, (held, first, second, *early[1:], early[0], profiles), (late[0],), [scratch, scratch, sems], name="lowest",
    )
    new_velocity, right_side = last(
        outer_kernel, (held, first, second, third, *late[2:], *late[:2], profiles), before,
        [scratch, scratch, margins, margins, sems], name="outer", input_output_aliases={9: 0, 10: 1},
    )
    return new_velocity, right_side


def solution(mesh):
    spec = P(None, None, "gz", "gx")
    return jax.shard_map(local, mesh=mesh, in_specs=(spec, spec), out_specs=(spec, spec), check_vma=False)
```
